256 devices in a mesh: dp: 16 (over x, y_lo, core), mp: 16 (over z, y_hi).
Axes of the slice: x: 4, y: 4 (y_hi: 2, y_lo: 2; y = y_hi * 2 + y_lo), z: 8, core: 2. Of those that a mesh axis runs over, the one named last changes fastest.
Arguments:
- tokens: bfloat16 [4096, 6144], P('dp'), may hold values from -6 to 6
- w_qkv: bfloat16 [6144, 3, 4096], P('dp', None, 'mp'), as said below
- w_out: bfloat16 [6144, 4096], P('dp', 'mp'), may hold values from -0.09375 to 0.09375
- layer_norm_gain: float32 [6144], replicated, may hold values from 0.1 to 1.9
- query_gain: float32 [4096], P('mp'), may hold values from 0.1 to 1.9
- key_gain: float32 [4096], P('mp'), may hold values from 0.1 to 1.9
- cotangent: bfloat16 [4096, 6144], P('dp'), may hold values from -6 to 6
Outputs:
- branch: bfloat16 [4096, 6144], P('dp', 'mp')
- token_gradient: bfloat16 [4096, 6144], P('dp', 'mp')
- grad_qkv_weight: bfloat16 [6144, 3, 4096], P('dp', None, 'mp')
- grad_out_weight: bfloat16 [6144, 4096], P('dp', 'mp')
The draws below stay inside these ranges and needn't reach their ends.
Inputs may be any that keep to these rules, and one draw needn't show every extreme that they name: `w_qkv`: entries are of order 6144^-0.5.
All inputs are finite; a program needn't handle non-finite values.
Results may differ from the reference program's by a relative error of at most 0.035.
Values may be sent and summed in bfloat16 or wider, within the bound.
No kernel may reach another device: no remote copies, remote signals or barrier semaphores. Data moves between devices by JAX's collectives and lax.ppermute only.
A program may use at most 128 MiB of HBM per device.

```python
import jax
import jax.numpy as jnp
from jax import lax

D = 6144
HEADS = 32
DH = 128
IMG_TOK = 256
TOK_DEV = 256
TOKENS = 4096
IMAGES = 16
N_DP = 16
N_MP = 16


def draw_w_qkv(key, part):
    key = jax.random.fold_in(key, 11)
    noise_key, column_key = jax.random.split(key)
    width = HEADS * DH
    noise = jnp.clip(jax.random.normal(noise_key, (D, 3, width), jnp.float32), -4.0, 4.0)
    rise = 4.0
    ramp = jnp.arange(D, dtype=jnp.float32) / (D - 1)
    row_scale = 0.5 * jnp.exp(ramp * jnp.log(rise))
    column_factor = jnp.clip(jax.random.normal(column_key, (1, 3, width), jnp.float32), -3.0, 3.0)
    weights = (noise + row_scale[:, None, None] * column_factor) * D ** (-0.5)
    return weights.astype(jnp.bfloat16)


def shard_levels(key, shape, pieces, smallest, high):
    factor_of = 1.0
    for axis_at, shards_of in pieces:
        steps = jax.random.uniform(jax.random.fold_in(jax.random.fold_in(key, 6), axis_at), (shards_of,), jnp.float32, smallest / len(pieces), high / len(pieces))
        factor_of = factor_of * jnp.repeat(jnp.exp(steps), shape[axis_at] // shards_of).reshape((-1,) + (1,) * (len(shape) - 1 - axis_at))
    return factor_of


def centred(key, shape, scale, bound, shards=(), kind=jnp.bfloat16):
    loudness = shard_levels(key, shape, shards, -0.22, 0.18) if shards else 1.0
    entries = jax.random.normal(key, shape, jnp.float32) * scale * loudness
    return jnp.minimum(jnp.maximum(entries, -bound), bound).astype(kind)


def setup_inputs(seed: int = 0) -> dict:
    arg_keys = jax.random.split(jax.random.key(seed), 8)
    tokens = centred(arg_keys[0], (TOKENS, D), 1.0, 6.0, ((0, 16),))
    w_qkv = draw_w_qkv(jax.random.fold_in(arg_keys[7], 71), 0)
    w_out = centred(arg_keys[2], (D, HEADS * DH), (HEADS * DH) ** -0.5, 0.09375, ((0, 16), (1, 16)))
    layer_norm_gain = jnp.clip(1.0 + 0.18 * jax.random.normal(arg_keys[3], (D,), jnp.float32), 0.1, 1.9)
    query_gain = jnp.clip(1.0 + 0.18 * jax.random.normal(arg_keys[4], (HEADS * DH,), jnp.float32), 0.1, 1.9)
    key_gain = jnp.clip(1.0 + 0.18 * jax.random.normal(arg_keys[5], (HEADS * DH,), jnp.float32), 0.1, 1.9)
    cotangent = centred(arg_keys[6], (TOKENS, D), 1.0, 6.0, ((0, 16),))
    return dict(tokens=tokens, w_qkv=w_qkv, w_out=w_out, layer_norm_gain=layer_norm_gain, query_gain=query_gain, key_gain=key_gain, cotangent=cotangent)


EPS = 1e-06

def rounded_values(values):
    return lax.optimization_barrier(values.astype(jnp.bfloat16))

def head_stats(values):
    centered_input = values - lax.optimization_barrier(jnp.mean(values, -1, keepdims=True))
    spread = lax.rsqrt(lax.optimization_barrier(jnp.mean(centered_input * centered_input, -1, keepdims=True)) + EPS)
    return (centered_input * spread, spread)

def head_back(grad, normed, spread, gain):
    scaled_input = grad * gain.reshape(HEADS, DH)
    return (scaled_input - lax.optimization_barrier(jnp.mean(scaled_input, -1, keepdims=True)) - normed * lax.optimization_barrier(jnp.mean(scaled_input * normed, -1, keepdims=True))) * spread

def per_image(values):
    return values.reshape(IMAGES, IMG_TOK, HEADS, DH).astype(jnp.float32)

def reference(tokens, w_qkv, w_out, layer_norm_gain, query_gain, key_gain, cotangent):
    width = HEADS * DH
    group = width // N_MP
    scale = DH ** (-0.5)
    features = tokens.astype(jnp.float32)
    centered_input = features - lax.optimization_barrier(jnp.mean(features, -1, keepdims=True))
    reciprocal_deviation = lax.rsqrt(lax.optimization_barrier(jnp.mean(centered_input * centered_input, -1, keepdims=True)) + EPS)
    normalized_input = centered_input * reciprocal_deviation
    hidden_state = rounded_values(normalized_input * layer_norm_gain)
    qkv = jnp.dot(hidden_state, w_qkv.reshape(D, 3 * width), preferred_element_type=jnp.float32).reshape(TOKENS, 3, HEADS, DH)
    query_normed, query_spread = head_stats(qkv[:, 0])
    key_normed, key_spread = head_stats(qkv[:, 1])
    queries = rounded_values(query_normed * query_gain.reshape(HEADS, DH))
    keys = rounded_values(key_normed * key_gain.reshape(HEADS, DH))
    values = rounded_values(qkv[:, 2])
    image_q = per_image(queries)
    image_k = per_image(keys)
    image_v = per_image(values)
    scores = jnp.einsum('bqhd,bkhd->bhqk', image_q, image_k) * scale
    expd = jnp.exp(scores)
    probs = expd / lax.optimization_barrier(jnp.sum(expd, -1, keepdims=True))
    pweights = rounded_values(probs).astype(jnp.float32)
    attended = rounded_values(jnp.einsum('bhqk,bkhd->bqhd', pweights, image_v)).reshape(TOKENS, width)

    def out_group(total, index):
        columns = lax.dynamic_slice_in_dim(attended, index * group, group, 1)
        weight_cols = lax.dynamic_slice_in_dim(w_out, index * group, group, 1)
        term = jnp.dot(columns, weight_cols.T, preferred_element_type=jnp.float32)
        return (total + rounded_values(term).astype(jnp.float32), None)
    branch_sum, _ = lax.scan(out_group, jnp.zeros((TOKENS, D), jnp.float32), jnp.arange(N_MP, dtype=jnp.int32))
    branch = branch_sum.astype(jnp.bfloat16)

    def out_grad_group(total, index):
        cot_rows = lax.dynamic_slice_in_dim(cotangent, index * TOK_DEV, TOK_DEV, 0)
        att_rows = lax.dynamic_slice_in_dim(attended, index * TOK_DEV, TOK_DEV, 0)
        term = jnp.dot(cot_rows.T, att_rows, preferred_element_type=jnp.float32)
        return (total + rounded_values(term).astype(jnp.float32), None)
    grad_out_sum, _ = lax.scan(out_grad_group, jnp.zeros((D, width), jnp.float32), jnp.arange(N_DP, dtype=jnp.int32))
    grad_out_weight = grad_out_sum.astype(jnp.bfloat16)
    grad_att = rounded_values(jnp.dot(cotangent, w_out, preferred_element_type=jnp.float32))
    image_grad = per_image(grad_att)
    grad_probs = jnp.einsum('bqhd,bkhd->bhqk', image_grad, image_v)
    delta = lax.optimization_barrier(jnp.sum(probs * grad_probs, -1, keepdims=True))
    grad_scores = rounded_values(probs * (grad_probs - delta) * scale).astype(jnp.float32)
    grad_qn = jnp.einsum('bhqk,bkhd->bqhd', grad_scores, image_k).reshape(TOKENS, HEADS, DH)
    grad_kn = jnp.einsum('bhqk,bqhd->bkhd', grad_scores, image_q).reshape(TOKENS, HEADS, DH)
    grad_values = jnp.einsum('bhqk,bqhd->bkhd', pweights, image_grad).reshape(TOKENS, HEADS, DH)
    grad_q = head_back(grad_qn, query_normed, query_spread, query_gain)
    grad_k = head_back(grad_kn, key_normed, key_spread, key_gain)
    grad_qkv = rounded_values(jnp.stack([grad_q, grad_k, grad_values], 1).reshape(TOKENS, 3, width))
    grad_flat = grad_qkv.reshape(TOKENS, 3 * width)

    def qkv_grad_group(total, index):
        hidden_rows = lax.dynamic_slice_in_dim(hidden_state, index * TOK_DEV, TOK_DEV, 0)
        grad_rows = lax.dynamic_slice_in_dim(grad_flat, index * TOK_DEV, TOK_DEV, 0)
        term = jnp.dot(hidden_rows.T, grad_rows, preferred_element_type=jnp.float32)
        return (total + rounded_values(term).astype(jnp.float32), None)
    grad_qkv_sum, _ = lax.scan(qkv_grad_group, jnp.zeros((D, 3 * width), jnp.float32), jnp.arange(N_DP, dtype=jnp.int32))
    grad_qkv_weight = grad_qkv_sum.reshape(D, 3, width).astype(jnp.bfloat16)

    def hidden_group(total, index):
        grad_part = lax.dynamic_slice_in_dim(grad_qkv, index * group, group, 2).reshape(TOKENS, 3 * group)
        weight_part = lax.dynamic_slice_in_dim(w_qkv, index * group, group, 2).reshape(D, 3 * group)
        term = jnp.dot(grad_part, weight_part.T, preferred_element_type=jnp.float32)
        return (total + rounded_values(term).astype(jnp.float32), None)
    grad_hidden, _ = lax.scan(hidden_group, jnp.zeros((TOKENS, D), jnp.float32), jnp.arange(N_MP, dtype=jnp.int32))
    scaled_input = grad_hidden * layer_norm_gain
    token_gradient = ((scaled_input - lax.optimization_barrier(jnp.mean(scaled_input, -1, keepdims=True)) - normalized_input * lax.optimization_barrier(jnp.mean(scaled_input * normalized_input, -1, keepdims=True))) * reciprocal_deviation).astype(jnp.bfloat16)
    return (branch, token_gradient, grad_qkv_weight, grad_out_weight)
```

```python
import jax
import jax.numpy as jnp
from jax import lax
from jax.experimental import pallas as pl
from jax.experimental.pallas import tpu as pltpu
from jax.sharding import Mesh, PartitionSpec as P

DH = 128
EPS = 1e-06
DP = ("x", "yl", "c")
MP = ("z", "yh")
NX, NYL, NC, NZ, NYH = 4, 2, 2, 8, 2
NDP, NMP = NX * NYL * NC, NZ * NYH
ROWS = 256
SL = 384
HW = 256
D = 6144
SUB = ROWS // NZ
STEP = 2
KSTEP = 4
VMEM = 52 * 1024 * 1024
BF = jnp.bfloat16
F32 = jnp.float32


def dot(a, b, ca, cb):
    return lax.dot_general(a, b, (((ca,), (cb,)), ((), ())), preferred_element_type=F32)


def params():
    return pltpu.CompilerParams(vmem_limit_bytes=VMEM)


def normalise(t):
    mean = jnp.mean(t, -1, keepdims=True)
    cen = t - mean
    rstd = lax.rsqrt(jnp.mean(cen * cen, -1, keepdims=True) + EPS)
    return cen * rstd, mean, rstd


def norm_kernel(tok_ref, gain_ref, hid_ref, mean_ref, rstd_ref):
    xhat, mean, rstd = normalise(tok_ref[...].astype(F32))
    hid_ref[...] = (xhat * gain_ref[...]).astype(BF)
    mean_ref[...] = mean
    rstd_ref[...] = rstd


def norm_call(tokens, gain):
    blk = 64
    return pl.pallas_call(
        norm_kernel,
        grid=(ROWS // blk,),
        in_specs=[
            pl.BlockSpec((blk, D), lambda i: (i, 0)),
            pl.BlockSpec((1, D), lambda i: (0, 0)),
        ],
        out_specs=[
            pl.BlockSpec((blk, D), lambda i: (i, 0)),
            pl.BlockSpec((blk, 1), lambda i: (i, 0)),
            pl.BlockSpec((blk, 1), lambda i: (i, 0)),
        ],
        out_shape=[
            jax.ShapeDtypeStruct((ROWS, D), BF),
            jax.ShapeDtypeStruct((ROWS, 1), F32),
            jax.ShapeDtypeStruct((ROWS, 1), F32),
        ],
        compiler_params=params(),
        cost_estimate=pl.CostEstimate(flops=2 * 10**7, bytes_accessed=2 * ROWS * D * 2, transcendentals=0),
    )(tokens, gain.reshape(1, D))


def rows_kernel(z_ref, tok_ref, cot_ref, gain_ref, out_ref):
    xhat, _, _ = normalise(tok_ref[...].astype(F32))
    hid = (xhat * gain_ref[...]).astype(BF)
    for i in range(NDP):
        out_ref[i, 0] = hid[:, i * SL : (i + 1) * SL]
        out_ref[i, 1] = cot_ref[:, i * SL : (i + 1) * SL]


def rows_call(z, tokens, cotangent, gain):
    return pl.pallas_call(
        rows_kernel,
        grid_spec=pltpu.PrefetchScalarGridSpec(
            num_scalar_prefetch=1,
            grid=(1,),
            in_specs=[
                pl.BlockSpec((SUB, D), lambda i, z: (z[0], 0)),
                pl.BlockSpec((SUB, D), lambda i, z: (z[0], 0)),
                pl.BlockSpec((1, D), lambda i, z: (0, 0)),
            ],
            out_specs=pl.BlockSpec((NDP, 2, SUB, SL), lambda i, z: (0, 0, 0, 0)),
        ),
        out_shape=jax.ShapeDtypeStruct((NDP, 2, SUB, SL), BF),
        compiler_params=params(),
        cost_estimate=pl.CostEstimate(flops=10**6, bytes_accessed=4 * SUB * D * 2, transcendentals=0),
    )(z, tokens, cotangent, gain.reshape(1, D))


def head_stats(u):
    cen = u - jnp.mean(u, -1, keepdims=True)
    s = lax.rsqrt(jnp.mean(cen * cen, -1, keepdims=True) + EPS)
    return cen * s, s


def head_back(g, n, s, gain):
    e = g * gain
    return (e - jnp.mean(e, -1, keepdims=True) - n * jnp.mean(e * n, -1, keepdims=True)) * s


def attn_kernel(hid_ref, cot_ref, w_ref, qg_ref, kg_ref, *rest):
    out_ref, acc, acc_g = rest[-3:]
    i = pl.program_id(0)

    @pl.when(i == 0)
    def _():
        acc[...] = jnp.zeros_like(acc)
        acc_g[...] = jnp.zeros_like(acc_g)

    h = hid_ref[...]
    for j in range(3):
        acc[j] += dot(h, w_ref[:, j].reshape(KSTEP * SL, HW), 1, 0)
    acc_g[...] += dot(cot_ref[...], w_ref[:, 3].reshape(KSTEP * SL, HW), 1, 0)

    @pl.when(i == pl.num_programs(0) - 1)
    def _():
        scale = DH ** (-0.5)
        for hd in range(HW // DH):
            sl = slice(hd * DH, (hd + 1) * DH)
            qg = qg_ref[:, sl]
            kg = kg_ref[:, sl]
            qn, qs = head_stats(acc[0, :, sl])
            kn, ks = head_stats(acc[1, :, sl])
            q = (qn * qg).astype(BF)
            k = (kn * kg).astype(BF)
            v = acc[2, :, sl].astype(BF)
            ga = acc_g[:, sl].astype(BF)
            e = jnp.exp(dot(q, k, 1, 1) * scale)
            p = e / jnp.sum(e, -1, keepdims=True)
            pw = p.astype(BF)
            att = dot(pw, v, 1, 0).astype(BF)
            gp = dot(ga, v, 1, 1)
            delta = jnp.sum(p * gp, -1, keepdims=True)
            gs = (p * (gp - delta) * scale).astype(BF)
            gq = head_back(dot(gs, k, 1, 0), qn, qs, qg)
            gk = head_back(dot(gs, q, 0, 0), kn, ks, kg)
            gv = dot(pw, ga, 0, 0)
            for j, val in enumerate((gq, gk, gv)):
                out_ref[:, j * HW + hd * DH : j * HW + (hd + 1) * DH] = val.astype(BF)
            out_ref[:, 3 * HW + hd * DH : 3 * HW + (hd + 1) * DH] = att


def attn_call(hid, cot, w, qg, kg, after):
    return pl.pallas_call(
        attn_kernel,
        grid=(NDP // KSTEP,),
        in_specs=[
            pl.BlockSpec((ROWS, KSTEP * SL), lambda i: (0, i)),
            pl.BlockSpec((ROWS, KSTEP * SL), lambda i: (0, i)),
            pl.BlockSpec((KSTEP, 4, SL, HW), lambda i: (i, 0, 0, 0)),
            pl.BlockSpec((1, HW), lambda i: (0, 0)),
            pl.BlockSpec((1, HW), lambda i: (0, 0)),
        ]
        + [pl.BlockSpec(memory_space=pl.ANY)] * len(after),
        out_specs=pl.BlockSpec((ROWS, 4 * HW), lambda i: (0, 0)),
        out_shape=jax.ShapeDtypeStruct((ROWS, 4 * HW), BF),
        scratch_shapes=[pltpu.VMEM((3, ROWS, HW), F32), pltpu.VMEM((ROWS, HW), F32)],
        compiler_params=params(),
        cost_estimate=pl.CostEstimate(
            flops=2 * ROWS * D * 4 * HW, bytes_accessed=20 * 10**6, transcendentals=ROWS * ROWS * 2
        ),
    )(hid, cot, w, qg.reshape(1, HW), kg.reshape(1, HW), *after)


def branch_kernel(g_ref, w_ref, out_ref):
    for s in range(STEP):
        out_ref[s] = dot(g_ref[...], w_ref[s, 0], 1, 1).astype(BF)


def branch_call(g, w):
    return pl.pallas_call(
        branch_kernel,
        grid=(NDP // STEP,),
        in_specs=[
            pl.BlockSpec((ROWS, HW), lambda i: (0, 3)),
            pl.BlockSpec((STEP, 1, SL, HW), lambda i: (i, 3, 0, 0)),
        ],
        out_specs=pl.BlockSpec((STEP, ROWS, SL), lambda i: (i, 0, 0)),
        out_shape=jax.ShapeDtypeStruct((NDP, ROWS, SL), BF),
        compiler_params=params(),
        cost_estimate=pl.CostEstimate(
            flops=2 * ROWS * D * HW, bytes_accessed=6 * 10**6, transcendentals=0
        ),
    )(g, w)


def back_kernel(g_ref, w_ref, hid_ref, gain_ref, *rest):
    hp_ref, sum_ref, s1, s2 = rest[-4:]
    i = pl.program_id(0)

    @pl.when(i == 0)
    def _():
        s1[...] = jnp.zeros_like(s1)
        s2[...] = jnp.zeros_like(s2)

    for s in range(STEP):
        t = dot(g_ref[:, :HW], w_ref[s, 0], 1, 1)
        t += dot(g_ref[:, HW : 2 * HW], w_ref[s, 1], 1, 1)
        t += dot(g_ref[:, 2 * HW :], w_ref[s, 2], 1, 1)
        hp_ref[s] = t.astype(BF)
        a = t * gain_ref[s]
        b = t * hid_ref[:, s * SL : (s + 1) * SL].astype(F32)
        for c in range(SL // 128):
            s1[...] += a[:, c * 128 : (c + 1) * 128]
            s2[...] += b[:, c * 128 : (c + 1) * 128]

    @pl.when(i == pl.num_programs(0) - 1)
    def _():
        sum_ref[:, 0:1] = jnp.sum(s1[...], -1, keepdims=True)
        sum_ref[:, 1:2] = jnp.sum(s2[...], -1, keepdims=True)


def back_call(g, w, hid, gain, after):
    return pl.pallas_call(
        back_kernel,
        grid=(NDP // STEP,),
        in_specs=[
            pl.BlockSpec((ROWS, 3 * HW), lambda i: (0, 0)),
            pl.BlockSpec((STEP, 3, SL, HW), lambda i: (i, 0, 0, 0)),
            pl.BlockSpec((ROWS, STEP * SL), lambda i: (0, i)),
            pl.BlockSpec((STEP, 1, SL), lambda i: (i, 0, 0)),
        ]
        + [pl.BlockSpec(memory_space=pl.ANY)] * len(after),
        out_specs=[
            pl.BlockSpec((STEP, ROWS, SL), lambda i: (i, 0, 0)),
            pl.BlockSpec((ROWS, 2), lambda i: (0, 0)),
        ],
        out_shape=[
            jax.ShapeDtypeStruct((NDP, ROWS, SL), BF),
            jax.ShapeDtypeStruct((ROWS, 2), F32),
        ],
        scratch_shapes=[pltpu.VMEM((ROWS, 128), F32), pltpu.VMEM((ROWS, 128), F32)],
        compiler_params=params(),
        cost_estimate=pl.CostEstimate(
            flops=2 * ROWS * D * 3 * HW, bytes_accessed=16 * 10**6, transcendentals=0
        ),
    )(g, w, hid, gain.reshape(NDP, 1, SL), *after)


def weight_kernel(z_ref, x_ref, g_ref, dw_ref, do_ref, acc, acc_o):
    i = pl.program_id(0)

    @pl.when(i == 0)
    def _():
        acc[...] = jnp.zeros_like(acc)
        acc_o[...] = jnp.zeros_like(acc_o)

    g = g_ref[...].reshape(NDP * SUB, 4 * HW)
    acc[...] += dot(x_ref[0, :, 0].reshape(NDP * SUB, SL), g[:, : 3 * HW], 0, 0)
    acc_o[...] += dot(x_ref[0, :, 1].reshape(NDP * SUB, SL), g[:, 3 * HW :], 0, 0)

    @pl.when(i == pl.num_programs(0) - 1)
    def _():
        for j in range(3):
            dw_ref[j] = acc[:, j * HW : (j + 1) * HW].astype(BF)
        do_ref[...] = acc_o[...].astype(BF)


def weight_call(z, x, g):
    return pl.pallas_call(
        weight_kernel,
        grid_spec=pltpu.PrefetchScalarGridSpec(
            num_scalar_prefetch=1,
            grid=(NZ,),
            in_specs=[
                pl.BlockSpec((1, NDP, 2, SUB, SL), lambda i, z: (i, 0, 0, 0, 0)),
                pl.BlockSpec((NDP, 1, SUB, 4 * HW), lambda i, z: (0, (z[0] + NZ - i) % NZ, 0, 0)),
            ],
            out_specs=[
                pl.BlockSpec((3, SL, HW), lambda i, z: (0, 0, 0)),
                pl.BlockSpec((SL, HW), lambda i, z: (0, 0)),
            ],
            scratch_shapes=[pltpu.VMEM((SL, 3 * HW), F32), pltpu.VMEM((SL, HW), F32)],
        ),
        out_shape=[
            jax.ShapeDtypeStruct((3, SL, HW), BF),
            jax.ShapeDtypeStruct((SL, HW), BF),
        ],
        compiler_params=params(),
        cost_estimate=pl.CostEstimate(
            flops=2 * ROWS * D * 4 * HW, bytes_accessed=16 * 10**6, transcendentals=0
        ),
    )(z, x, g.reshape(NDP, NZ, SUB, 4 * HW))


def shift(a, k):
    return lax.ppermute(a, "z", [(i, (i + k) % NZ) for i in range(NZ)])


def swap_yh(a):
    return lax.ppermute(a, "yh", [(0, 1), (1, 0)])


def ring_gather(own):
    half = NDP // 2
    r1, l1 = shift(own, 1), shift(own, -1)
    r2, l2 = shift(r1, 1), shift(l1, -1)
    r3, l3 = shift(r2, 1), shift(l2, -1)
    far = jnp.concatenate([shift(r3[:half], 1), shift(l3[half:], -1)], 0)
    return jnp.stack([own, r1, r2, r3, far, l3, l2, l1], 0), (r3, l3)


def ring_sum(a, z):
    a = a.reshape(NZ, NYH, ROWS, SL)

    def block(k):
        return lax.dynamic_index_in_dim(a, lax.rem(z + k + NZ, NZ), 0, keepdims=False)

    far = block(4)
    p = shift(far[0], 1)
    m = shift(far[1], -1)
    u, v = block(3), block(-3)
    p = shift(jnp.stack([u[0] + p, u[1]]), 1)
    m = shift(jnp.stack([v[0], v[1] + m]), -1)
    p, m = shift(block(2) + p, 1), shift(block(-2) + m, -1)
    p, m = shift(block(1) + p, 1), shift(block(-1) + m, -1)
    return block(0).astype(F32) + p.astype(F32) + m.astype(F32)


def all_sum(a):
    x = jnp.broadcast_to(a.T[None], (NMP, 2, ROWS))
    return jnp.sum(lax.all_to_all(x, MP, 0, 0, tiled=True), 0)


def across(part, yh):
    mine = lax.dynamic_index_in_dim(part, yh, 0, keepdims=False)
    other = lax.dynamic_index_in_dim(part, 1 - yh, 0, keepdims=False)
    return mine.astype(F32) + swap_yh(other.astype(BF)).astype(F32)


def local(tokens, w_qkv, w_out, layer_norm_gain, query_gain, key_gain, cotangent):
    z = lax.axis_index("z")
    yh = lax.axis_index("yh")
    zs = z.reshape(1).astype(jnp.int32)
    col = (z * NYH + yh) * SL

    w_own = jnp.concatenate([w_qkv.transpose(1, 0, 2), w_out[None]], 0)
    w = lax.all_gather(w_own, DP, axis=0)
    side = lax.psum_scatter(w_own, "c", scatter_dimension=0, tiled=True)

    rows = rows_call(zs, tokens, cotangent, layer_norm_gain)
    rows, early = ring_gather(lax.all_to_all(rows, DP, 0, 0, tiled=True))
    hid, mean, rstd = norm_call(tokens, layer_norm_gain)

    grads = attn_call(hid, cotangent, w, query_gain, key_gain, early + (side,))
    all_grads = lax.all_gather(grads, DP, axis=0)
    branch_terms = branch_call(grads, w)
    branch_part = lax.psum_scatter(
        branch_terms.reshape(NDP * ROWS, SL), "z", scatter_dimension=0, tiled=True
    ).reshape(NYH, ROWS, SL)
    hidden_terms, sums = back_call(grads, w, hid, layer_norm_gain, (rows,))
    sums = all_sum(sums) / D
    grad_hidden = across(ring_sum(hidden_terms, z), yh)
    branch = across(branch_part, yh).astype(BF)

    gain = lax.dynamic_slice_in_dim(layer_norm_gain, col, SL, 0)
    toks = lax.dynamic_slice_in_dim(tokens, col, SL, 1).astype(F32)
    xhat = (toks - mean) * rstd
    token_gradient = (
        (grad_hidden * gain - sums[0][:, None] - xhat * sums[1][:, None]) * rstd
    ).astype(BF)

    grad_w, grad_o = weight_call(zs, rows, all_grads)
    return (branch, token_gradient, grad_w.transpose(1, 0, 2), grad_o)


def solution(mesh):
    fine = Mesh(mesh.devices.reshape(NX, NYL, NC, NZ, NYH), DP + MP)
    return jax.shard_map(
        local,
        mesh=fine,
        in_specs=(
            P(DP, None),
            P(DP, None, MP),
            P(DP, MP),
            P(),
            P(MP),
            P(MP),
            P(DP, None),
        ),
        out_specs=(P(DP, MP), P(DP, MP), P(DP, None, MP), P(DP, MP)),
        check_vma=False,
    )
```

```python
import jax
import jax.numpy as jnp
from jax import lax
from jax.experimental import pallas as pl
from jax.experimental.pallas import tpu as pltpu
from jax.sharding import Mesh, PartitionSpec as P

DH = 128
EPS = 1e-06
DP = ("x", "yl", "c")
MP = ("z", "yh")
NX, NYL, NC, NZ, NYH = 4, 2, 2, 8, 2
NDP, NMP = NX * NYL * NC, NZ * NYH
ROWS = 256
SL = 384
HW = 256
D = 6144
SUB = ROWS // NZ
EXT = ROWS + 16
STEP = 4
KSTEP = 4
COST = pl.CostEstimate(flops=1000, bytes_accessed=1000, transcendentals=0)
VMEM = 52 * 1024 * 1024
BF = jnp.bfloat16
F32 = jnp.float32


def dot(a, b, ca, cb):
    return lax.dot_general(a, b, (((ca,), (cb,)), ((), ())), preferred_element_type=F32)


def params():
    return pltpu.CompilerParams(vmem_limit_bytes=VMEM)


ANY = pl.BlockSpec(memory_space=pl.ANY)


def order(xs, after):
    n = len(xs)
    return pl.pallas_call(
        lambda *refs: None,
        in_specs=[ANY] * (n + len(after)),
        out_specs=[ANY] * n,
        out_shape=[jax.ShapeDtypeStruct(x.shape, x.dtype) for x in xs],
        input_output_aliases={i: i for i in range(n)},
        cost_estimate=COST,
    )(*xs, *after)


def normalise(t):
    mean = jnp.mean(t, -1, keepdims=True)
    cen = t - mean
    rstd = lax.rsqrt(jnp.mean(cen * cen, -1, keepdims=True) + EPS)
    return cen * rstd, mean, rstd


def norm_kernel(tok_ref, gain_ref, hid_ref, mean_ref, rstd_ref):
    i = pl.program_id(0)
    blk = tok_ref.shape[0]
    gain = gain_ref[...]
    xhat, mean, rstd = normalise(tok_ref[...].astype(F32))
    hid_ref[pl.ds(pl.multiple_of(i * blk, blk), blk), :] = (xhat * gain).astype(BF)
    mean_ref[...] = mean
    rstd_ref[...] = rstd

    @pl.when(i == pl.num_programs(0) - 1)
    def _():
        hi = gain.astype(BF).astype(F32)
        row = lax.broadcasted_iota(jnp.int32, (16, D), 0)
        extra = jnp.where(row == 0, hi, jnp.where(row == 1, gain - hi, 0.0))
        hid_ref[ROWS:, :] = extra.astype(BF)


def norm_call(tokens, gain):
    blk = 64
    return pl.pallas_call(
        norm_kernel,
        grid=(ROWS // blk,),
        in_specs=[
            pl.BlockSpec((blk, D), lambda i: (i, 0)),
            pl.BlockSpec((1, D), lambda i: (0, 0)),
        ],
        out_specs=[
            pl.BlockSpec((EXT, D), lambda i: (0, 0)),
            pl.BlockSpec((blk, 1), lambda i: (i, 0)),
            pl.BlockSpec((blk, 1), lambda i: (i, 0)),
        ],
        out_shape=[
            jax.ShapeDtypeStruct((EXT, D), BF),
            jax.ShapeDtypeStruct((ROWS, 1), F32),
            jax.ShapeDtypeStruct((ROWS, 1), F32),
        ],
        compiler_params=params(),
        cost_estimate=COST,
    )(tokens, gain.reshape(1, D))


def rows_kernel(z_ref, tok_ref, cot_ref, gain_ref, out_ref):
    xhat, _, _ = normalise(tok_ref[...].astype(F32))
    hid = (xhat * gain_ref[...]).astype(BF)
    for i in range(NDP):
        out_ref[i, 0] = hid[:, i * SL : (i + 1) * SL]
        out_ref[i, 1] = cot_ref[:, i * SL : (i + 1) * SL]


def rows_call(z, tokens, cotangent, gain):
    return pl.pallas_call(
        rows_kernel,
        grid_spec=pltpu.PrefetchScalarGridSpec(
            num_scalar_prefetch=1,
            grid=(1,),
            in_specs=[
                pl.BlockSpec((SUB, D), lambda i, z: (z[0], 0)),
                pl.BlockSpec((SUB, D), lambda i, z: (z[0], 0)),
                pl.BlockSpec((1, D), lambda i, z: (0, 0)),
            ],
            out_specs=pl.BlockSpec((NDP, 2, SUB, SL), lambda i, z: (0, 0, 0, 0)),
        ),
        out_shape=jax.ShapeDtypeStruct((NDP, 2, SUB, SL), BF),
        compiler_params=params(),
        cost_estimate=COST,
    )(z, tokens, cotangent, gain.reshape(1, D))


def head_stats(u):
    cen = u - jnp.mean(u, -1, keepdims=True)
    s = lax.rsqrt(jnp.mean(cen * cen, -1, keepdims=True) + EPS)
    return cen * s, s


def head_back(g, n, s, gain):
    e = g * gain
    return (e - jnp.mean(e, -1, keepdims=True) - n * jnp.mean(e * n, -1, keepdims=True)) * s


def proj_kernel(hid_ref, cot_ref, w_ref, *rest):
    out_ref = rest[-1]
    i = pl.program_id(0)
    cols = pl.ds(pl.multiple_of(i * KSTEP * SL, KSTEP * SL), KSTEP * SL)
    h = hid_ref[:, cols]
    c = cot_ref[:, cols]
    for j in range(4):
        rows = EXT if j < 3 else ROWS
        new = dot(h if j < 3 else c, w_ref[:, j].reshape(KSTEP * SL, HW), 1, 0)

        @pl.when(i == 0)
        def _():
            out_ref[:rows, j * HW : (j + 1) * HW] = new

        @pl.when(i > 0)
        def _():
            out_ref[:rows, j * HW : (j + 1) * HW] += new


def proj_call(hid, cot, w, after):
    return pl.pallas_call(
        proj_kernel,
        grid=(NDP // KSTEP,),
        in_specs=[pl.BlockSpec(memory_space=pltpu.VMEM)] * 2
        + [pl.BlockSpec((KSTEP, 4, SL, HW), lambda i: (i, 0, 0, 0))]
        + [ANY] * len(after),
        out_specs=pl.BlockSpec((EXT, 4 * HW), lambda i: (0, 0)),
        out_shape=jax.ShapeDtypeStruct((EXT, 4 * HW), F32),
        compiler_params=params(),
        cost_estimate=COST,
    )(hid, cot, w, *after)


def attn_kernel(acc_ref, qg_ref, kg_ref, *rest):
    out_ref, sum_ref = rest[-2:]
    scale = DH ** (-0.5)
    t1 = jnp.zeros((ROWS, DH), F32)
    t2 = jnp.zeros((ROWS, DH), F32)
    for hd in range(HW // DH):
        cols = [slice(j * HW + hd * DH, j * HW + (hd + 1) * DH) for j in range(4)]
        sl = cols[0]
        qg = qg_ref[:, sl]
        kg = kg_ref[:, sl]
        proj = [acc_ref[:ROWS, c] for c in cols]
        qn, qs = head_stats(proj[0])
        kn, ks = head_stats(proj[1])
        q = (qn * qg).astype(BF)
        k = (kn * kg).astype(BF)
        v = proj[2].astype(BF)
        ga = proj[3].astype(BF)
        e = jnp.exp(dot(q, k, 1, 1) * scale)
        p = e / jnp.sum(e, -1, keepdims=True)
        pw = p.astype(BF)
        out_ref[:, cols[3]] = dot(pw, v, 1, 0).astype(BF)
        gp = dot(ga, v, 1, 1)
        delta = jnp.sum(p * gp, -1, keepdims=True)
        gs = (p * (gp - delta) * scale).astype(BF)
        gq = head_back(dot(gs, k, 1, 0), qn, qs, qg)
        gk = head_back(dot(gs, q, 0, 0), kn, ks, kg)
        gv = dot(pw, ga, 0, 0)
        for j, val in enumerate((gq, gk, gv)):
            g = val.astype(BF)
            out_ref[:, cols[j]] = g
            g = g.astype(F32)
            t1 += g * (acc_ref[ROWS : ROWS + 1, cols[j]] + acc_ref[ROWS + 1 : ROWS + 2, cols[j]])
            t2 += g * proj[j]
    ones = jnp.ones((8, DH), F32)
    total = [
        lax.dot_general(
            ones, t, (((1,), (1,)), ((), ())), precision=lax.Precision.HIGHEST, preferred_element_type=F32
        )
        for t in (t1, t2)
    ]
    row = lax.broadcasted_iota(jnp.int32, (8, ROWS), 0)
    sum_ref[...] = jnp.where(row == 0, total[0], total[1])


def attn_call(acc, qg, kg, after):
    full = lambda shape: pl.BlockSpec(shape, lambda: (0, 0))
    return pl.pallas_call(
        attn_kernel,
        in_specs=[full((EXT, 4 * HW)), full((1, HW)), full((1, HW))]
        + [pl.BlockSpec(memory_space=pl.ANY)] * len(after),
        out_specs=[full((ROWS, 4 * HW)), full((8, ROWS))],
        out_shape=[
            jax.ShapeDtypeStruct((ROWS, 4 * HW), BF),
            jax.ShapeDtypeStruct((8, ROWS), F32),
        ],
        compiler_params=params(),
        cost_estimate=COST,
    )(acc, qg.reshape(1, HW), kg.reshape(1, HW), *after)


def back_kernel(g_ref, w_ref, out_ref):
    for s in range(STEP):
        t = dot(g_ref[:, :HW], w_ref[s, 0], 1, 1)
        t += dot(g_ref[:, HW : 2 * HW], w_ref[s, 1], 1, 1)
        t += dot(g_ref[:, 2 * HW : 3 * HW], w_ref[s, 2], 1, 1)
        out_ref[s, :ROWS] = t.astype(BF)
        out_ref[s, ROWS:] = dot(g_ref[:, 3 * HW :], w_ref[s, 3], 1, 1).astype(BF)


def back_call(g, w):
    return pl.pallas_call(
        back_kernel,
        grid=(NDP // STEP,),
        in_specs=[
            pl.BlockSpec((ROWS, 4 * HW), lambda i: (0, 0)),
            pl.BlockSpec((STEP, 4, SL, HW), lambda i: (i, 0, 0, 0)),
        ],
        out_specs=pl.BlockSpec((STEP, 2 * ROWS, SL), lambda i: (i, 0, 0)),
        out_shape=jax.ShapeDtypeStruct((NDP, 2 * ROWS, SL), BF),
        compiler_params=params(),
        cost_estimate=COST,
    )(g, w)


def weight_kernel(part, z_ref, *refs):
    x_refs, rest = refs[:NZ], refs[NZ:]
    g_refs = rest[:2]
    i = pl.program_id(0)
    half = NDP // 2
    n = half * SUB

    def total(step):
        new, new_o = 0.0, 0.0
        for k in (0, 1):
            for h in (0, 1):
                x = x_refs[2 * (2 * step + k) + h]
                g = g_refs[k][h * half : (h + 1) * half].reshape(n, 4 * HW)
                new = new + dot(x[:, 0].reshape(n, SL), g[:, : 3 * HW], 0, 0)
                new_o = new_o + dot(x[:, 1].reshape(n, SL), g[:, 3 * HW :], 0, 0)
        return new, new_o

    if part == 0:
        acc, acc_o = rest[2:4]

        @pl.when(i == 0)
        def _():
            acc[...], acc_o[...] = total(0)

        @pl.when(i == 1)
        def _():
            new, new_o = total(1)
            acc[...] += new
            acc_o[...] += new_o
    else:
        old, old_o, dw_ref, do_ref, acc, acc_o = rest[2:8]

        @pl.when(i == 0)
        def _():
            new, new_o = total(0)
            acc[...] = old[...] + new
            acc_o[...] = old_o[...] + new_o

        @pl.when(i == 1)
        def _():
            new, new_o = total(1)
            for j in range(3):
                sl = slice(j * HW, (j + 1) * HW)
                dw_ref[j] = (acc[:, sl] + new[:, sl]).astype(BF)
            do_ref[...] = (acc_o[...] + new_o).astype(BF)


def weight_call(part, scalars, xs, g, old):
    g = g.reshape(NDP, NZ, SUB, 4 * HW)
    shapes = [(SL, 3 * HW), (SL, HW)]
    outs = [(3, SL, HW), (SL, HW)]
    zero = lambda n: (lambda i, z: (0,) * n)
    spot = lambda k: (lambda i, z: (0, (z[0] + 2 * NZ - 4 * part - 2 * i - k) % NZ, 0, 0))
    out = outs if part else shapes
    return pl.pallas_call(
        lambda *refs: weight_kernel(part, *refs),
        grid_spec=pltpu.PrefetchScalarGridSpec(
            num_scalar_prefetch=1,
            grid=(2,),
            in_specs=[pl.BlockSpec(x.shape, zero(4)) for x in xs]
            + [pl.BlockSpec((NDP, 1, SUB, 4 * HW), spot(k)) for k in (0, 1)]
            + [pl.BlockSpec(x.shape, zero(2)) for x in old],
            out_specs=[pl.BlockSpec(x, zero(len(x))) for x in out],
            scratch_shapes=[pltpu.VMEM(x, F32) for x in shapes] if part else [],
        ),
        out_shape=[jax.ShapeDtypeStruct(x, BF if part else F32) for x in out],
        compiler_params=params(),
        cost_estimate=COST,
    )(scalars, *xs, g, g, *old)


def shift(a, k):
    return lax.ppermute(a, "z", [(i, (i + k) % NZ) for i in range(NZ)])


def swap_yh(a):
    return lax.ppermute(a, "yh", [(0, 1), (1, 0)])


def ring_gather(own, hid):
    half = NDP // 2
    a, b = own[:half], own[half:]
    ra, la, rb, lb = order((shift(a, 1), shift(a, -1), shift(b, 1), shift(b, -1)), (hid,))
    right, left = [(ra, rb)], [(la, lb)]
    for _ in range(2):
        right.append(tuple(shift(x, 1) for x in right[-1]))
        left.append(tuple(shift(x, -1) for x in left[-1]))
    far = shift(right[-1][0], 1), shift(left[-1][1], -1)
    return [(a, b)] + right + [far] + left[::-1]


def all_sum(a):
    x = jnp.broadcast_to(a[None], (NMP,) + a.shape)
    return jnp.sum(lax.all_to_all(x, MP, 0, 0, tiled=True), 0)


def final_kernel(s_ref, mine_ref, recv_ref, sum_ref, tok_ref, mean_ref, rstd_ref, gain_ref, *refs):
    branch_ref, token_ref = refs[-2:]
    t = mine_ref[0].astype(F32) + recv_ref[...].astype(F32)
    s = jnp.transpose(sum_ref[...]) * (1.0 / D)
    rstd = rstd_ref[...]
    xhat = (tok_ref[...].astype(F32) - mean_ref[...]) * rstd
    grad = t[:ROWS] * gain_ref[...] - s[:, 0:1] - xhat * s[:, 1:2]
    token_ref[...] = (grad * rstd).astype(BF)
    branch_ref[...] = t[ROWS:].astype(BF)


def final_call(scalars, part, recv, sums, tokens, mean, rstd, gain, after):
    fixed = lambda i, s: (0, 0)
    cols = lambda i, s: (0, s[2])
    out = jax.ShapeDtypeStruct((ROWS, SL), BF)
    return pl.pallas_call(
        final_kernel,
        grid_spec=pltpu.PrefetchScalarGridSpec(
            num_scalar_prefetch=1,
            grid=(1,),
            in_specs=[
                pl.BlockSpec((1, 2 * ROWS, SL), lambda i, s: (s[1], 0, 0)),
                pl.BlockSpec((2 * ROWS, SL), fixed),
                pl.BlockSpec((8, ROWS), fixed),
                pl.BlockSpec((ROWS, SL), cols),
                pl.BlockSpec((ROWS, 1), fixed),
                pl.BlockSpec((ROWS, 1), fixed),
                pl.BlockSpec((1, SL), cols),
            ]
            + [ANY] * len(after),
            out_specs=[pl.BlockSpec((ROWS, SL), fixed)] * 2,
        ),
        out_shape=[out, out],
        compiler_params=params(),
        cost_estimate=COST,
    )(scalars, part, recv, sums, tokens, mean, rstd, gain.reshape(1, D), *after)


def local(tokens, w_qkv, w_out, layer_norm_gain, query_gain, key_gain, cotangent):
    z = lax.axis_index("z")
    yh = lax.axis_index("yh")
    scalars = jnp.stack([z, yh, z * NYH + yh]).astype(jnp.int32)

    w_own = jnp.concatenate([w_qkv.transpose(1, 0, 2), w_out[None]], 0)
    w = lax.all_gather(w_own, DP, axis=0)
    side = lax.psum_scatter(w_own, "c", scatter_dimension=0, tiled=True)

    hid, mean, rstd = norm_call(tokens, layer_norm_gain)
    rows = rows_call(scalars, tokens, cotangent, layer_norm_gain)
    moved = ring_gather(lax.all_to_all(rows, DP, 0, 0, tiled=True), hid)

    acc = proj_call(hid, cotangent, w, moved[2] + moved[6] + (side,))
    grads, sums = attn_call(acc, query_gain, key_gain, moved[3] + moved[4] + moved[5])
    all_grads = lax.all_gather(grads, DP, axis=0)
    terms = back_call(grads, w)
    part = lax.psum_scatter(
        terms.reshape(NDP * 2 * ROWS, SL), "z", scatter_dimension=0, tiled=True
    ).reshape(NYH, 2 * ROWS, SL)
    sums = all_sum(sums)
    flat = [x for pair in moved for x in pair]
    partial = weight_call(0, scalars, flat[:NZ], all_grads, ())
    grad_w, grad_o = weight_call(1, scalars, flat[NZ:], all_grads, partial)
    (part,) = order((part,), (grad_w, sums))
    recv = swap_yh(lax.dynamic_index_in_dim(part, 1 - yh, 0, keepdims=False))
    branch, token_gradient = final_call(
        scalars, part, recv, sums, tokens, mean, rstd, layer_norm_gain, ()
    )
    return (branch, token_gradient, grad_w.transpose(1, 0, 2), grad_o)


def solution(mesh):
    fine = Mesh(mesh.devices.reshape(NX, NYL, NC, NZ, NYH), DP + MP)
    return jax.shard_map(
        local,
        mesh=fine,
        in_specs=(
            P(DP, None),
            P(DP, None, MP),
            P(DP, MP),
            P(),
            P(MP),
            P(MP),
            P(DP, None),
        ),
        out_specs=(P(DP, MP), P(DP, MP), P(DP, None, MP), P(DP, MP)),
        check_vma=False,
    )
```

```python
import jax
import jax.numpy as jnp
from jax import lax
from jax.experimental import pallas as pl
from jax.experimental.pallas import tpu as pltpu
from jax.sharding import Mesh, PartitionSpec as P

DH = 128
EPS = 1e-06
DP = ("x", "yl", "c")
MP = ("z", "yh")
NX, NYL, NC, NZ, NYH = 4, 2, 2, 8, 2
NDP, NMP = NX * NYL * NC, NZ * NYH
ROWS = 256
SL = 384
HW = 256
D = 6144
SUB = ROWS // NZ
EXT = ROWS + 16
KSTEP = 4
COST = pl.CostEstimate(flops=1000, bytes_accessed=1000, transcendentals=0)
VMEM = 52 * 1024 * 1024
BF = jnp.bfloat16
F32 = jnp.float32


def dot(a, b, ca, cb):
    return lax.dot_general(a, b, (((ca,), (cb,)), ((), ())), preferred_element_type=F32)


def params():
    return pltpu.CompilerParams(vmem_limit_bytes=VMEM)


ANY = pl.BlockSpec(memory_space=pl.ANY)


def order(xs, after):
    n = len(xs)
    return pl.pallas_call(
        lambda *refs: None,
        in_specs=[ANY] * (n + len(after)),
        out_specs=[ANY] * n,
        out_shape=[jax.ShapeDtypeStruct(x.shape, x.dtype) for x in xs],
        input_output_aliases={i: i for i in range(n)},
        cost_estimate=COST,
    )(*xs, *after)


def normalise(t):
    mean = jnp.mean(t, -1, keepdims=True)
    cen = t - mean
    rstd = lax.rsqrt(jnp.mean(cen * cen, -1, keepdims=True) + EPS)
    return cen * rstd, mean, rstd


def norm_kernel(tok_ref, gain_ref, hid_ref, mean_ref, rstd_ref):
    i = pl.program_id(0)
    blk = tok_ref.shape[0]
    gain = gain_ref[...]
    xhat, mean, rstd = normalise(tok_ref[...].astype(F32))
    hid_ref[pl.ds(pl.multiple_of(i * blk, blk), blk), :] = (xhat * gain).astype(BF)
    mean_ref[...] = mean
    rstd_ref[...] = rstd

    @pl.when(i == pl.num_programs(0) - 1)
    def _():
        hi = gain.astype(BF).astype(F32)
        row = lax.broadcasted_iota(jnp.int32, (16, D), 0)
        extra = jnp.where(row == 0, hi, jnp.where(row == 1, gain - hi, 0.0))
        hid_ref[ROWS:, :] = extra.astype(BF)


def norm_call(tokens, gain):
    blk = 64
    return pl.pallas_call(
        norm_kernel,
        grid=(ROWS // blk,),
        in_specs=[
            pl.BlockSpec((blk, D), lambda i: (i, 0)),
            pl.BlockSpec((1, D), lambda i: (0, 0)),
        ],
        out_specs=[
            pl.BlockSpec((EXT, D), lambda i: (0, 0)),
            pl.BlockSpec((blk, 1), lambda i: (i, 0)),
            pl.BlockSpec((blk, 1), lambda i: (i, 0)),
        ],
        out_shape=[
            jax.ShapeDtypeStruct((EXT, D), BF),
            jax.ShapeDtypeStruct((ROWS, 1), F32),
            jax.ShapeDtypeStruct((ROWS, 1), F32),
        ],
        compiler_params=params(),
        cost_estimate=COST,
    )(tokens, gain.reshape(1, D))


def rows_kernel(z_ref, tok_ref, cot_ref, gain_ref, out_ref):
    xhat, _, _ = normalise(tok_ref[...].astype(F32))
    hid = (xhat * gain_ref[...]).astype(BF)
    for i in range(NDP):
        out_ref[i, 0] = hid[:, i * SL : (i + 1) * SL]
        out_ref[i, 1] = cot_ref[:, i * SL : (i + 1) * SL]


def rows_call(z, tokens, cotangent, gain):
    return pl.pallas_call(
        rows_kernel,
        grid_spec=pltpu.PrefetchScalarGridSpec(
            num_scalar_prefetch=1,
            grid=(1,),
            in_specs=[
                pl.BlockSpec((SUB, D), lambda i, z: (z[0], 0)),
                pl.BlockSpec((SUB, D), lambda i, z: (z[0], 0)),
                pl.BlockSpec((1, D), lambda i, z: (0, 0)),
            ],
            out_specs=pl.BlockSpec((NDP, 2, SUB, SL), lambda i, z: (0, 0, 0, 0)),
        ),
        out_shape=jax.ShapeDtypeStruct((NDP, 2, SUB, SL), BF),
        compiler_params=params(),
        cost_estimate=COST,
    )(z, tokens, cotangent, gain.reshape(1, D))


def head_stats(u):
    cen = u - jnp.mean(u, -1, keepdims=True)
    s = lax.rsqrt(jnp.mean(cen * cen, -1, keepdims=True) + EPS)
    return cen * s, s


def head_back(g, n, s, gain):
    e = g * gain
    return (e - jnp.mean(e, -1, keepdims=True) - n * jnp.mean(e * n, -1, keepdims=True)) * s


def attn_kernel(acc_ref, qg_ref, kg_ref, *rest):
    out_ref, sum_ref = rest[-2:]
    scale = DH ** (-0.5)
    t1 = jnp.zeros((ROWS, DH), F32)
    t2 = jnp.zeros((ROWS, DH), F32)
    for hd in range(HW // DH):
        cols = [slice(j * HW + hd * DH, j * HW + (hd + 1) * DH) for j in range(4)]
        sl = cols[0]
        qg = qg_ref[:, sl]
        kg = kg_ref[:, sl]
        proj = [acc_ref[:ROWS, c] for c in cols]
        qn, qs = head_stats(proj[0])
        kn, ks = head_stats(proj[1])
        q = (qn * qg).astype(BF)
        k = (kn * kg).astype(BF)
        v = proj[2].astype(BF)
        ga = proj[3].astype(BF)
        e = jnp.exp(dot(q, k, 1, 1) * scale)
        p = e / jnp.sum(e, -1, keepdims=True)
        pw = p.astype(BF)
        out_ref[:, cols[3]] = dot(pw, v, 1, 0).astype(BF)
        gp = dot(ga, v, 1, 1)
        delta = jnp.sum(p * gp, -1, keepdims=True)
        gs = (p * (gp - delta) * scale).astype(BF)
        gq = head_back(dot(gs, k, 1, 0), qn, qs, qg)
        gk = head_back(dot(gs, q, 0, 0), kn, ks, kg)
        gv = dot(pw, ga, 0, 0)
        for j, val in enumerate((gq, gk, gv)):
            g = val.astype(BF)
            out_ref[:, cols[j]] = g
            g = g.astype(F32)
            t1 += g * (acc_ref[ROWS : ROWS + 1, cols[j]] + acc_ref[ROWS + 1 : ROWS + 2, cols[j]])
            t2 += g * proj[j]
    ones = jnp.ones((8, DH), F32)
    total = [
        lax.dot_general(
            ones, t, (((1,), (1,)), ((), ())), precision=lax.Precision.HIGHEST, preferred_element_type=F32
        )
        for t in (t1, t2)
    ]
    row = lax.broadcasted_iota(jnp.int32, (8, ROWS), 0)
    sum_ref[...] = jnp.where(row == 0, total[0], total[1])


def core_kernel(hid_in, cot_in, w_in, qg_ref, kg_ref, *rest):
    g_ref, sum_ref, out_ref, hid, cot, w, acc, out, sems, out_sems = rest[-10:]
    groups = NDP // KSTEP
    loads = []
    for i in range(groups):
        cols = slice(i * KSTEP * SL, (i + 1) * KSTEP * SL)
        span = slice(i * KSTEP, (i + 1) * KSTEP)
        pairs = [
            (hid_in.at[:, cols], hid.at[:, cols]),
            (cot_in.at[:, cols], cot.at[:, cols]),
            (w_in.at[span], w.at[span]),
        ]
        loads.append([pltpu.make_async_copy(a, b, sems.at[i, n]) for n, (a, b) in enumerate(pairs)])
    for group in loads:
        for copy in group:
            copy.start()
    for i, group in enumerate(loads):
        for copy in group:
            copy.wait()
        cols = slice(i * KSTEP * SL, (i + 1) * KSTEP * SL)
        for j in range(4):
            rows = EXT if j < 3 else ROWS
            src = hid if j < 3 else cot
            wj = w[i * KSTEP : (i + 1) * KSTEP, j].reshape(KSTEP * SL, HW)
            new = dot(src[:, cols], wj, 1, 0)
            dst = slice(j * HW, (j + 1) * HW)
            acc[:rows, dst] = new if i == 0 else acc[:rows, dst] + new
    attn_kernel(acc, qg_ref, kg_ref, g_ref, sum_ref)
    stores = []
    for i in range(groups):
        for s in range(i * KSTEP, (i + 1) * KSTEP):
            t = 0.0
            for j in range(3):
                t = t + dot(g_ref[:, j * HW : (j + 1) * HW], w[s, j], 1, 1)
            out[s, :ROWS] = t.astype(BF)
            out[s, ROWS:] = dot(g_ref[:, 3 * HW :], w[s, 3], 1, 1).astype(BF)
        span = slice(i * KSTEP, (i + 1) * KSTEP)
        stores.append(pltpu.make_async_copy(out.at[span], out_ref.at[span], out_sems.at[i]))
        stores[-1].start()
    for copy in stores:
        copy.wait()


def core_call(hid, cot, w, qg, kg, after):
    full = lambda shape: pl.BlockSpec(shape, lambda: (0, 0))
    groups = NDP // KSTEP
    return pl.pallas_call(
        core_kernel,
        in_specs=[ANY] * 3 + [full((1, HW)), full((1, HW))] + [ANY] * len(after),
        out_specs=[full((ROWS, 4 * HW)), full((8, ROWS)), ANY],
        out_shape=[
            jax.ShapeDtypeStruct((ROWS, 4 * HW), BF),
            jax.ShapeDtypeStruct((8, ROWS), F32),
            jax.ShapeDtypeStruct((NDP, 2 * ROWS, SL), BF),
        ],
        scratch_shapes=[
            pltpu.VMEM((EXT, D), BF),
            pltpu.VMEM((ROWS, D), BF),
            pltpu.VMEM((NDP, 4, SL, HW), BF),
            pltpu.VMEM((EXT, 4 * HW), F32),
            pltpu.VMEM((NDP, 2 * ROWS, SL), BF),
            pltpu.SemaphoreType.DMA((groups, 3)),
            pltpu.SemaphoreType.DMA((groups,)),
        ],
        compiler_params=params(),
        cost_estimate=COST,
    )(hid, cot, w, qg.reshape(1, HW), kg.reshape(1, HW), *after)


def weight_kernel(part, z_ref, *refs):
    x_refs, rest = refs[:NZ], refs[NZ:]
    g_refs = rest[:2]
    i = pl.program_id(0)
    half = NDP // 2
    n = half * SUB

    def total(step):
        new, new_o = 0.0, 0.0
        for k in (0, 1):
            for h in (0, 1):
                x = x_refs[2 * (2 * step + k) + h]
                g = g_refs[k][h * half : (h + 1) * half].reshape(n, 4 * HW)
                new = new + dot(x[:, 0].reshape(n, SL), g[:, : 3 * HW], 0, 0)
                new_o = new_o + dot(x[:, 1].reshape(n, SL), g[:, 3 * HW :], 0, 0)
        return new, new_o

    if part == 0:
        acc, acc_o = rest[2:4]

        @pl.when(i == 0)
        def _():
            acc[...], acc_o[...] = total(0)

        @pl.when(i == 1)
        def _():
            new, new_o = total(1)
            acc[...] += new
            acc_o[...] += new_o
    else:
        old, old_o, dw_ref, do_ref, acc, acc_o = rest[2:8]

        @pl.when(i == 0)
        def _():
            new, new_o = total(0)
            acc[...] = old[...] + new
            acc_o[...] = old_o[...] + new_o

        @pl.when(i == 1)
        def _():
            new, new_o = total(1)
            for j in range(3):
                sl = slice(j * HW, (j + 1) * HW)
                dw_ref[j] = (acc[:, sl] + new[:, sl]).astype(BF)
            do_ref[...] = (acc_o[...] + new_o).astype(BF)


def weight_call(part, scalars, xs, g, old):
    g = g.reshape(NDP, NZ, SUB, 4 * HW)
    shapes = [(SL, 3 * HW), (SL, HW)]
    outs = [(3, SL, HW), (SL, HW)]
    zero = lambda n: (lambda i, z: (0,) * n)
    spot = lambda k: (lambda i, z: (0, (z[0] + 2 * NZ - 4 * part - 2 * i - k) % NZ, 0, 0))
    out = outs if part else shapes
    return pl.pallas_call(
        lambda *refs: weight_kernel(part, *refs),
        grid_spec=pltpu.PrefetchScalarGridSpec(
            num_scalar_prefetch=1,
            grid=(2,),
            in_specs=[pl.BlockSpec(x.shape, zero(4)) for x in xs]
            + [pl.BlockSpec((NDP, 1, SUB, 4 * HW), spot(k)) for k in (0, 1)]
            + [pl.BlockSpec(x.shape, zero(2)) for x in old],
            out_specs=[pl.BlockSpec(x, zero(len(x))) for x in out],
            scratch_shapes=[pltpu.VMEM(x, F32) for x in shapes] if part else [],
        ),
        out_shape=[jax.ShapeDtypeStruct(x, BF if part else F32) for x in out],
        compiler_params=params(),
        cost_estimate=COST,
    )(scalars, *xs, g, g, *old)


def shift(a, k):
    return lax.ppermute(a, "z", [(i, (i + k) % NZ) for i in range(NZ)])


def swap_yh(a):
    return lax.ppermute(a, "yh", [(0, 1), (1, 0)])


def ring_gather(own, hid):
    half = NDP // 2
    a, b = own[:half], own[half:]
    ra, la = order((shift(a, 1), shift(a, -1)), (hid,))
    right, left = [(ra, shift(b, 1))], [(la, shift(b, -1))]
    for _ in range(2):
        right.append(tuple(shift(x, 1) for x in right[-1]))
        left.append(tuple(shift(x, -1) for x in left[-1]))
    return [(a, b)] + right + left[::-1]


def all_sum(a):
    x = jnp.broadcast_to(a[None], (NMP,) + a.shape)
    return jnp.sum(lax.all_to_all(x, MP, 0, 0, tiled=True), 0)


def final_kernel(s_ref, mine_ref, recv_ref, sum_ref, tok_ref, mean_ref, rstd_ref, gain_ref, *refs):
    branch_ref, token_ref = refs[-2:]
    t = mine_ref[0].astype(F32) + recv_ref[...].astype(F32)
    s = jnp.transpose(sum_ref[...]) * (1.0 / D)
    rstd = rstd_ref[...]
    xhat = (tok_ref[...].astype(F32) - mean_ref[...]) * rstd
    grad = t[:ROWS] * gain_ref[...] - s[:, 0:1] - xhat * s[:, 1:2]
    token_ref[...] = (grad * rstd).astype(BF)
    branch_ref[...] = t[ROWS:].astype(BF)


def final_call(scalars, part, recv, sums, tokens, mean, rstd, gain, after):
    fixed = lambda i, s: (0, 0)
    cols = lambda i, s: (0, s[2])
    out = jax.ShapeDtypeStruct((ROWS, SL), BF)
    return pl.pallas_call(
        final_kernel,
        grid_spec=pltpu.PrefetchScalarGridSpec(
            num_scalar_prefetch=1,
            grid=(1,),
            in_specs=[
                pl.BlockSpec((1, 2 * ROWS, SL), lambda i, s: (s[1], 0, 0)),
                pl.BlockSpec((2 * ROWS, SL), fixed),
                pl.BlockSpec((8, ROWS), fixed),
                pl.BlockSpec((ROWS, SL), cols),
                pl.BlockSpec((ROWS, 1), fixed),
                pl.BlockSpec((ROWS, 1), fixed),
                pl.BlockSpec((1, SL), cols),
            ]
            + [ANY] * len(after),
            out_specs=[pl.BlockSpec((ROWS, SL), fixed)] * 2,
        ),
        out_shape=[out, out],
        compiler_params=params(),
        cost_estimate=COST,
    )(scalars, part, recv, sums, tokens, mean, rstd, gain.reshape(1, D), *after)


def local(tokens, w_qkv, w_out, layer_norm_gain, query_gain, key_gain, cotangent):
    z = lax.axis_index("z")
    yh = lax.axis_index("yh")
    scalars = jnp.stack([z, yh, z * NYH + yh]).astype(jnp.int32)

    w_own = jnp.concatenate([w_qkv.transpose(1, 0, 2), w_out[None]], 0)
    w = lax.all_gather(w_own, DP, axis=0)
    side = lax.psum_scatter(w_own, "c", scatter_dimension=0, tiled=True)

    hid, mean, rstd = norm_call(tokens, layer_norm_gain)
    rows = rows_call(scalars, tokens, cotangent, layer_norm_gain)
    moved = ring_gather(lax.all_to_all(rows, DP, 0, 0, tiled=True), hid)

    (ra, rb), (la, lb) = moved[3], moved[4]
    grads, sums, terms = core_call(
        hid, cotangent, w, query_gain, key_gain, moved[3] + moved[4] + (side,)
    )
    all_grads = lax.all_gather(grads, DP, axis=0)
    part = lax.psum_scatter(
        terms.reshape(NDP * 2 * ROWS, SL), "z", scatter_dimension=0, tiled=True
    ).reshape(NYH, 2 * ROWS, SL)
    sums = all_sum(sums)
    ra, lb = order((ra, lb), (terms,))
    flat = [x for pair in moved[:3] for x in pair] + [ra, rb]
    flat += [shift(ra, 1), shift(lb, -1), la, lb] + [x for pair in moved[5:] for x in pair]
    partial = weight_call(0, scalars, flat[:NZ], all_grads, ())
    grad_w, grad_o = weight_call(1, scalars, flat[NZ:], all_grads, partial)
    (part,) = order((part,), (grad_w, sums))
    recv = swap_yh(lax.dynamic_index_in_dim(part, 1 - yh, 0, keepdims=False))
    branch, token_gradient = final_call(
        scalars, part, recv, sums, tokens, mean, rstd, layer_norm_gain, ()
    )
    return (branch, token_gradient, grad_w.transpose(1, 0, 2), grad_o)


def solution(mesh):
    fine = Mesh(mesh.devices.reshape(NX, NYL, NC, NZ, NYH), DP + MP)
    return jax.shard_map(
        local,
        mesh=fine,
        in_specs=(
            P(DP, None),
            P(DP, None, MP),
            P(DP, MP),
            P(),
            P(MP),
            P(MP),
            P(DP, None),
        ),
        out_specs=(P(DP, MP), P(DP, MP), P(DP, None, MP), P(DP, MP)),
        check_vma=False,
    )
```

```python
import jax
import jax.numpy as jnp
from jax import lax
from jax.experimental import pallas as pl
from jax.experimental.pallas import tpu as pltpu
from jax.sharding import Mesh, PartitionSpec as P

DH = 128
EPS = 1e-06
DP = ("x", "yl", "c")
MP = ("z", "yh")
NX, NYL, NC, NZ, NYH = 4, 2, 2, 8, 2
NDP, NMP = NX * NYL * NC, NZ * NYH
ROWS = 256
SL = 384
HW = 256
D = 6144
SUB = ROWS // NZ
EXT = ROWS + 16
KSTEP = 4
COST = pl.CostEstimate(flops=1000, bytes_accessed=1000, transcendentals=0)
VMEM = 52 * 1024 * 1024
BF = jnp.bfloat16
F32 = jnp.float32


def dot(a, b, ca, cb):
    return lax.dot_general(a, b, (((ca,), (cb,)), ((), ())), preferred_element_type=F32)


def params():
    return pltpu.CompilerParams(vmem_limit_bytes=VMEM)


ANY = pl.BlockSpec(memory_space=pl.ANY)


def order(xs, after):
    n = len(xs)
    return pl.pallas_call(
        lambda *refs: None,
        in_specs=[ANY] * (n + len(after)),
        out_specs=[ANY] * n,
        out_shape=[jax.ShapeDtypeStruct(x.shape, x.dtype) for x in xs],
        input_output_aliases={i: i for i in range(n)},
        cost_estimate=COST,
    )(*xs, *after)


def normalise(t):
    mean = jnp.mean(t, -1, keepdims=True)
    cen = t - mean
    rstd = lax.rsqrt(jnp.mean(cen * cen, -1, keepdims=True) + EPS)
    return cen * rstd, mean, rstd


def norm_kernel(tok_ref, gain_ref, hid_ref, mean_ref, rstd_ref):
    i = pl.program_id(0)
    blk = tok_ref.shape[0]
    gain = gain_ref[...]
    xhat, mean, rstd = normalise(tok_ref[...].astype(F32))
    hid_ref[pl.ds(pl.multiple_of(i * blk, blk), blk), :] = (xhat * gain).astype(BF)
    mean_ref[...] = mean
    rstd_ref[...] = rstd

    @pl.when(i == pl.num_programs(0) - 1)
    def _():
        hi = gain.astype(BF).astype(F32)
        row = lax.broadcasted_iota(jnp.int32, (16, D), 0)
        extra = jnp.where(row == 0, hi, jnp.where(row == 1, gain - hi, 0.0))
        hid_ref[ROWS:, :] = extra.astype(BF)


def norm_call(tokens, gain):
    blk = 64
    return pl.pallas_call(
        norm_kernel,
        grid=(ROWS // blk,),
        in_specs=[
            pl.BlockSpec((blk, D), lambda i: (i, 0)),
            pl.BlockSpec((1, D), lambda i: (0, 0)),
        ],
        out_specs=[
            pl.BlockSpec((EXT, D), lambda i: (0, 0)),
            pl.BlockSpec((blk, 1), lambda i: (i, 0)),
            pl.BlockSpec((blk, 1), lambda i: (i, 0)),
        ],
        out_shape=[
            jax.ShapeDtypeStruct((EXT, D), BF),
            jax.ShapeDtypeStruct((ROWS, 1), F32),
            jax.ShapeDtypeStruct((ROWS, 1), F32),
        ],
        compiler_params=params(),
        cost_estimate=COST,
    )(tokens, gain.reshape(1, D))


def rows_kernel(z_ref, tok_ref, cot_ref, gain_ref, out_ref):
    xhat, _, _ = normalise(tok_ref[...].astype(F32))
    hid = (xhat * gain_ref[...]).astype(BF)
    for i in range(NDP):
        out_ref[i, 0] = hid[:, i * SL : (i + 1) * SL]
        out_ref[i, 1] = cot_ref[:, i * SL : (i + 1) * SL]


def rows_call(z, tokens, cotangent, gain):
    return pl.pallas_call(
        rows_kernel,
        grid_spec=pltpu.PrefetchScalarGridSpec(
            num_scalar_prefetch=1,
            grid=(1,),
            in_specs=[
                pl.BlockSpec((SUB, D), lambda i, z: (z[0], 0)),
                pl.BlockSpec((SUB, D), lambda i, z: (z[0], 0)),
                pl.BlockSpec((1, D), lambda i, z: (0, 0)),
            ],
            out_specs=pl.BlockSpec((NDP, 2, SUB, SL), lambda i, z: (0, 0, 0, 0)),
        ),
        out_shape=jax.ShapeDtypeStruct((NDP, 2, SUB, SL), BF),
        compiler_params=params(),
        cost_estimate=COST,
    )(z, tokens, cotangent, gain.reshape(1, D))


def head_stats(u):
    cen = u - jnp.mean(u, -1, keepdims=True)
    s = lax.rsqrt(jnp.mean(cen * cen, -1, keepdims=True) + EPS)
    return cen * s, s


def head_back(g, n, s, gain):
    e = g * gain
    return (e - jnp.mean(e, -1, keepdims=True) - n * jnp.mean(e * n, -1, keepdims=True)) * s


def attn_kernel(acc_ref, qg_ref, kg_ref, *rest):
    out_ref, sum_ref = rest[-2:]
    scale = DH ** (-0.5)
    t1 = jnp.zeros((ROWS, DH), F32)
    t2 = jnp.zeros((ROWS, DH), F32)
    for hd in range(HW // DH):
        cols = [slice(j * HW + hd * DH, j * HW + (hd + 1) * DH) for j in range(4)]
        sl = cols[0]
        qg = qg_ref[:, sl]
        kg = kg_ref[:, sl]
        proj = [acc_ref[:ROWS, c] for c in cols]
        qn, qs = head_stats(proj[0])
        kn, ks = head_stats(proj[1])
        q = (qn * qg).astype(BF)
        k = (kn * kg).astype(BF)
        v = proj[2].astype(BF)
        ga = proj[3].astype(BF)
        e = jnp.exp(dot(q, k, 1, 1) * scale)
        p = e / jnp.sum(e, -1, keepdims=True)
        pw = p.astype(BF)
        out_ref[:, cols[3]] = dot(pw, v, 1, 0).astype(BF)
        gp = dot(ga, v, 1, 1)
        delta = jnp.sum(p * gp, -1, keepdims=True)
        gs = (p * (gp - delta) * scale).astype(BF)
        gq = head_back(dot(gs, k, 1, 0), qn, qs, qg)
        gk = head_back(dot(gs, q, 0, 0), kn, ks, kg)
        gv = dot(pw, ga, 0, 0)
        for j, val in enumerate((gq, gk, gv)):
            g = val.astype(BF)
            out_ref[:, cols[j]] = g
            g = g.astype(F32)
            t1 += g * (acc_ref[ROWS : ROWS + 1, cols[j]] + acc_ref[ROWS + 1 : ROWS + 2, cols[j]])
            t2 += g * proj[j]
    ones = jnp.ones((8, DH), F32)
    total = [
        lax.dot_general(
            ones, t, (((1,), (1,)), ((), ())), precision=lax.Precision.HIGHEST, preferred_element_type=F32
        )
        for t in (t1, t2)
    ]
    row = lax.broadcasted_iota(jnp.int32, (8, ROWS), 0)
    sum_ref[...] = jnp.where(row == 0, total[0], total[1])


def core_kernel(hid_in, cot_in, w_in, qg_ref, kg_ref, *rest):
    g_ref, sum_ref, out_ref, hid, cot, w, acc, out, sems, out_sems = rest[-10:]
    groups = NDP // KSTEP
    loads = []
    for i in range(groups):
        cols = slice(i * KSTEP * SL, (i + 1) * KSTEP * SL)
        span = slice(i * KSTEP, (i + 1) * KSTEP)
        pairs = [
            (hid_in.at[:, cols], hid.at[:, cols]),
            (cot_in.at[:, cols], cot.at[:, cols]),
            (w_in.at[span], w.at[span]),
        ]
        loads.append([pltpu.make_async_copy(a, b, sems.at[i, n]) for n, (a, b) in enumerate(pairs)])
    for group in loads:
        for copy in group:
            copy.start()
    for i, group in enumerate(loads):
        for copy in group:
            copy.wait()
        cols = slice(i * KSTEP * SL, (i + 1) * KSTEP * SL)
        for j in range(4):
            rows = EXT if j < 3 else ROWS
            src = hid if j < 3 else cot
            wj = w[i * KSTEP : (i + 1) * KSTEP, j].reshape(KSTEP * SL, HW)
            new = dot(src[:, cols], wj, 1, 0)
            dst = slice(j * HW, (j + 1) * HW)
            acc[:rows, dst] = new if i == 0 else acc[:rows, dst] + new
    attn_kernel(acc, qg_ref, kg_ref, g_ref, sum_ref)
    stores = []
    for i in range(groups):
        for s in range(i * KSTEP, (i + 1) * KSTEP):
            t = 0.0
            for j in range(3):
                t = t + dot(g_ref[:, j * HW : (j + 1) * HW], w[s, j], 1, 1)
            out[s, :ROWS] = t.astype(BF)
            out[s, ROWS:] = dot(g_ref[:, 3 * HW :], w[s, 3], 1, 1).astype(BF)
        span = slice(i * KSTEP, (i + 1) * KSTEP)
        stores.append(pltpu.make_async_copy(out.at[span], out_ref.at[span], out_sems.at[i]))
        stores[-1].start()
    for copy in stores:
        copy.wait()


def core_call(hid, cot, w, qg, kg, after):
    full = lambda shape: pl.BlockSpec(shape, lambda: (0, 0))
    groups = NDP // KSTEP
    return pl.pallas_call(
        core_kernel,
        in_specs=[ANY] * 3 + [full((1, HW)), full((1, HW))] + [ANY] * len(after),
        out_specs=[full((ROWS, 4 * HW)), full((8, ROWS)), ANY],
        out_shape=[
            jax.ShapeDtypeStruct((ROWS, 4 * HW), BF),
            jax.ShapeDtypeStruct((8, ROWS), F32),
            jax.ShapeDtypeStruct((NDP, 2 * ROWS, SL), BF),
        ],
        scratch_shapes=[
            pltpu.VMEM((EXT, D), BF),
            pltpu.VMEM((ROWS, D), BF),
            pltpu.VMEM((NDP, 4, SL, HW), BF),
            pltpu.VMEM((EXT, 4 * HW), F32),
            pltpu.VMEM((NDP, 2 * ROWS, SL), BF),
            pltpu.SemaphoreType.DMA((groups, 3)),
            pltpu.SemaphoreType.DMA((groups,)),
        ],
        compiler_params=params(),
        cost_estimate=COST,
    )(hid, cot, w, qg.reshape(1, HW), kg.reshape(1, HW), *after)


def weight_kernel(part, z_ref, *refs):
    x_refs, rest = refs[:NZ], refs[NZ:]
    g_refs = rest[:2]
    i = pl.program_id(0)
    half = NDP // 2
    n = half * SUB

    def total(step):
        new, new_o = 0.0, 0.0
        for k in (0, 1):
            for h in (0, 1):
                x = x_refs[2 * (2 * step + k) + h]
                g = g_refs[k][h * half : (h + 1) * half].reshape(n, 4 * HW)
                new = new + dot(x[:, 0].reshape(n, SL), g[:, : 3 * HW], 0, 0)
                new_o = new_o + dot(x[:, 1].reshape(n, SL), g[:, 3 * HW :], 0, 0)
        return new, new_o

    if part == 0:
        acc, acc_o = rest[2:4]

        @pl.when(i == 0)
        def _():
            acc[...], acc_o[...] = total(0)

        @pl.when(i == 1)
        def _():
            new, new_o = total(1)
            acc[...] += new
            acc_o[...] += new_o
    else:
        old, old_o, dw_ref, do_ref, acc, acc_o = rest[2:8]

        @pl.when(i == 0)
        def _():
            new, new_o = total(0)
            acc[...] = old[...] + new
            acc_o[...] = old_o[...] + new_o

        @pl.when(i == 1)
        def _():
            new, new_o = total(1)
            for j in range(3):
                sl = slice(j * HW, (j + 1) * HW)
                dw_ref[j] = (acc[:, sl] + new[:, sl]).astype(BF)
            do_ref[...] = (acc_o[...] + new_o).astype(BF)


def weight_call(part, scalars, xs, g, old):
    g = g.reshape(NDP, NZ, SUB, 4 * HW)
    shapes = [(SL, 3 * HW), (SL, HW)]
    outs = [(3, SL, HW), (SL, HW)]
    zero = lambda n: (lambda i, z: (0,) * n)
    spot = lambda k: (lambda i, z: (0, (z[0] + 2 * NZ - 4 * part - 2 * i - k) % NZ, 0, 0))
    out = outs if part else shapes
    return pl.pallas_call(
        lambda *refs: weight_kernel(part, *refs),
        grid_spec=pltpu.PrefetchScalarGridSpec(
            num_scalar_prefetch=1,
            grid=(2,),
            in_specs=[pl.BlockSpec(x.shape, zero(4)) for x in xs]
            + [pl.BlockSpec((NDP, 1, SUB, 4 * HW), spot(k)) for k in (0, 1)]
            + [pl.BlockSpec(x.shape, zero(2)) for x in old],
            out_specs=[pl.BlockSpec(x, zero(len(x))) for x in out],
            scratch_shapes=[pltpu.VMEM(x, F32) for x in shapes] if part else [],
        ),
        out_shape=[jax.ShapeDtypeStruct(x, BF if part else F32) for x in out],
        compiler_params=params(),
        cost_estimate=COST,
    )(scalars, *xs, g, g, *old)


def shift(a, k):
    return lax.ppermute(a, "z", [(i, (i + k) % NZ) for i in range(NZ)])


def swap_yh(a):
    return lax.ppermute(a, "yh", [(0, 1), (1, 0)])


def ring_gather(own, hid):
    half = NDP // 2
    a, b = own[:half], own[half:]
    ra, la = order((shift(a, 1), shift(a, -1)), (hid,))
    right, left = [(ra, shift(b, 1))], [(la, shift(b, -1))]
    for _ in range(2):
        right.append(tuple(shift(x, 1) for x in right[-1]))
        left.append(tuple(shift(x, -1) for x in left[-1]))
    return [(a, b)] + right + left[::-1]


def all_sum(a):
    x = jnp.broadcast_to(a[None], (NMP,) + a.shape)
    return jnp.sum(lax.all_to_all(x, MP, 0, 0, tiled=True), 0)


def final_kernel(s_ref, mine_ref, recv_ref, sum_ref, tok_ref, mean_ref, rstd_ref, gain_ref, *refs):
    branch_ref, token_ref = refs[-2:]
    t = mine_ref[0].astype(F32) + recv_ref[...].astype(F32)
    s = jnp.transpose(sum_ref[...]) * (1.0 / D)
    rstd = rstd_ref[...]
    xhat = (tok_ref[...].astype(F32) - mean_ref[...]) * rstd
    grad = t[:ROWS] * gain_ref[...] - s[:, 0:1] - xhat * s[:, 1:2]
    token_ref[...] = (grad * rstd).astype(BF)
    branch_ref[...] = t[ROWS:].astype(BF)


def final_call(scalars, part, recv, sums, tokens, mean, rstd, gain, after):
    fixed = lambda i, s: (0, 0)
    cols = lambda i, s: (0, s[2])
    out = jax.ShapeDtypeStruct((ROWS, SL), BF)
    return pl.pallas_call(
        final_kernel,
        grid_spec=pltpu.PrefetchScalarGridSpec(
            num_scalar_prefetch=1,
            grid=(1,),
            in_specs=[
                pl.BlockSpec((1, 2 * ROWS, SL), lambda i, s: (s[1], 0, 0)),
                pl.BlockSpec((2 * ROWS, SL), fixed),
                pl.BlockSpec((8, ROWS), fixed),
                pl.BlockSpec((ROWS, SL), cols),
                pl.BlockSpec((ROWS, 1), fixed),
                pl.BlockSpec((ROWS, 1), fixed),
                pl.BlockSpec((1, SL), cols),
            ]
            + [ANY] * len(after),
            out_specs=[pl.BlockSpec((ROWS, SL), fixed)] * 2,
        ),
        out_shape=[out, out],
        compiler_params=params(),
        cost_estimate=COST,
    )(scalars, part, recv, sums, tokens, mean, rstd, gain.reshape(1, D), *after)


def local(tokens, w_qkv, w_out, layer_norm_gain, query_gain, key_gain, cotangent):
    z = lax.axis_index("z")
    yh = lax.axis_index("yh")
    scalars = jnp.stack([z, yh, z * NYH + yh]).astype(jnp.int32)

    w_own = jnp.concatenate([w_qkv.transpose(1, 0, 2), w_out[None]], 0)
    w = lax.all_gather(w_own, DP, axis=0)
    side = lax.psum_scatter(w_own, "c", scatter_dimension=0, tiled=True)

    hid, mean, rstd = norm_call(tokens, layer_norm_gain)
    rows = rows_call(scalars, tokens, cotangent, layer_norm_gain)
    moved = ring_gather(lax.all_to_all(rows, DP, 0, 0, tiled=True), hid)

    (ra, rb), (la, lb) = moved[3], moved[4]
    grads, sums, terms = core_call(
        hid, cotangent, w, query_gain, key_gain, moved[2] + moved[5] + (ra, lb, side)
    )
    far = shift(ra, 1), shift(lb, -1)
    terms, grads, sums = order((terms, grads, sums), far + (rb, la))
    all_grads = lax.all_gather(grads, DP, axis=0)
    part = lax.psum_scatter(
        terms.reshape(NDP * 2 * ROWS, SL), "z", scatter_dimension=0, tiled=True
    ).reshape(NYH, 2 * ROWS, SL)
    sums = all_sum(sums)
    flat = [x for pair in moved[:3] for x in pair] + [ra, rb]
    flat += [*far, la, lb] + [x for pair in moved[5:] for x in pair]
    partial = weight_call(0, scalars, flat[:NZ], all_grads, ())
    grad_w, grad_o = weight_call(1, scalars, flat[NZ:], all_grads, partial)
    (part,) = order((part,), (grad_w, sums))
    recv = swap_yh(lax.dynamic_index_in_dim(part, 1 - yh, 0, keepdims=False))
    branch, token_gradient = final_call(
        scalars, part, recv, sums, tokens, mean, rstd, layer_norm_gain, ()
    )
    return (branch, token_gradient, grad_w.transpose(1, 0, 2), grad_o)


def solution(mesh):
    fine = Mesh(mesh.devices.reshape(NX, NYL, NC, NZ, NYH), DP + MP)
    return jax.shard_map(
        local,
        mesh=fine,
        in_specs=(
            P(DP, None),
            P(DP, None, MP),
            P(DP, MP),
            P(),
            P(MP),
            P(MP),
            P(DP, None),
        ),
        out_specs=(P(DP, MP), P(DP, MP), P(DP, None, MP), P(DP, MP)),
        check_vma=False,
    )
```

```python
import jax
import jax.numpy as jnp
from jax import lax
from jax.experimental import pallas as pl
from jax.experimental.pallas import tpu as pltpu
from jax.sharding import Mesh, PartitionSpec as P

DH = 128
EPS = 1e-06
DP = ("x", "yl", "c")
MP = ("z", "yh")
NX, NYL, NC, NZ, NYH = 4, 2, 2, 8, 2
NDP, NMP = NX * NYL * NC, NZ * NYH
ROWS = 256
SL = 384
HW = 256
D = 6144
SUB = ROWS // NZ
EXT = ROWS + 16
KSTEP = 4
COST = pl.CostEstimate(flops=1000, bytes_accessed=1000, transcendentals=0)
VMEM = 52 * 1024 * 1024
BF = jnp.bfloat16
F32 = jnp.float32


def dot(a, b, ca, cb):
    return lax.dot_general(a, b, (((ca,), (cb,)), ((), ())), preferred_element_type=F32)


def params():
    return pltpu.CompilerParams(vmem_limit_bytes=VMEM)


ANY = pl.BlockSpec(memory_space=pl.ANY)


def order(xs, after):
    n = len(xs)
    return pl.pallas_call(
        lambda *refs: None,
        in_specs=[ANY] * (n + len(after)),
        out_specs=[ANY] * n,
        out_shape=[jax.ShapeDtypeStruct(x.shape, x.dtype) for x in xs],
        input_output_aliases={i: i for i in range(n)},
        cost_estimate=COST,
    )(*xs, *after)


def pack_kernel(a_ref, b_ref, out_ref, sems):
    copies = [pltpu.make_async_copy(a_ref.at[j], out_ref.at[j], sems.at[j]) for j in range(3)]
    copies.append(pltpu.make_async_copy(b_ref, out_ref.at[3], sems.at[3]))
    for copy in copies:
        copy.start()
    for copy in copies:
        copy.wait()


def pack_call(w_qkv, w_out):
    return pl.pallas_call(
        pack_kernel,
        in_specs=[ANY, ANY],
        out_specs=ANY,
        out_shape=jax.ShapeDtypeStruct((4, SL, HW), BF),
        scratch_shapes=[pltpu.SemaphoreType.DMA((4,))],
        compiler_params=params(),
        cost_estimate=COST,
    )(w_qkv.transpose(1, 0, 2), w_out)


def normalise(t):
    mean = jnp.mean(t, -1, keepdims=True)
    cen = t - mean
    rstd = lax.rsqrt(jnp.mean(cen * cen, -1, keepdims=True) + EPS)
    return cen * rstd, mean, rstd


def norm_kernel(tok_ref, gain_ref, hid_ref, mean_ref, rstd_ref):
    i = pl.program_id(0)
    blk = tok_ref.shape[0]
    gain = gain_ref[...]
    xhat, mean, rstd = normalise(tok_ref[...].astype(F32))
    hid_ref[pl.ds(pl.multiple_of(i * blk, blk), blk), :] = (xhat * gain).astype(BF)
    mean_ref[...] = mean
    rstd_ref[...] = rstd

    @pl.when(i == pl.num_programs(0) - 1)
    def _():
        hi = gain.astype(BF).astype(F32)
        row = lax.broadcasted_iota(jnp.int32, (16, D), 0)
        extra = jnp.where(row == 0, hi, jnp.where(row == 1, gain - hi, 0.0))
        hid_ref[ROWS:, :] = extra.astype(BF)


def norm_call(tokens, gain):
    blk = 64
    return pl.pallas_call(
        norm_kernel,
        grid=(ROWS // blk,),
        in_specs=[
            pl.BlockSpec((blk, D), lambda i: (i, 0)),
            pl.BlockSpec((1, D), lambda i: (0, 0)),
        ],
        out_specs=[
            pl.BlockSpec((EXT, D), lambda i: (0, 0)),
            pl.BlockSpec((blk, 1), lambda i: (i, 0)),
            pl.BlockSpec((blk, 1), lambda i: (i, 0)),
        ],
        out_shape=[
            jax.ShapeDtypeStruct((EXT, D), BF),
            jax.ShapeDtypeStruct((ROWS, 1), F32),
            jax.ShapeDtypeStruct((ROWS, 1), F32),
        ],
        compiler_params=params(),
        cost_estimate=COST,
    )(tokens, gain.reshape(1, D))


def rows_kernel(z_ref, tok_ref, cot_ref, gain_ref, out_ref):
    xhat, _, _ = normalise(tok_ref[...].astype(F32))
    hid = (xhat * gain_ref[...]).astype(BF)
    for i in range(NDP):
        out_ref[i, 0] = hid[:, i * SL : (i + 1) * SL]
        out_ref[i, 1] = cot_ref[:, i * SL : (i + 1) * SL]


def rows_call(z, tokens, cotangent, gain):
    return pl.pallas_call(
        rows_kernel,
        grid_spec=pltpu.PrefetchScalarGridSpec(
            num_scalar_prefetch=1,
            grid=(1,),
            in_specs=[
                pl.BlockSpec((SUB, D), lambda i, z: (z[0], 0)),
                pl.BlockSpec((SUB, D), lambda i, z: (z[0], 0)),
                pl.BlockSpec((1, D), lambda i, z: (0, 0)),
            ],
            out_specs=pl.BlockSpec((NDP, 2, SUB, SL), lambda i, z: (0, 0, 0, 0)),
        ),
        out_shape=jax.ShapeDtypeStruct((NDP, 2, SUB, SL), BF),
        compiler_params=params(),
        cost_estimate=COST,
    )(z, tokens, cotangent, gain.reshape(1, D))


def head_stats(u):
    cen = u - jnp.mean(u, -1, keepdims=True)
    s = lax.rsqrt(jnp.mean(cen * cen, -1, keepdims=True) + EPS)
    return cen * s, s


def head_back(g, n, s, gain):
    e = g * gain
    return (e - jnp.mean(e, -1, keepdims=True) - n * jnp.mean(e * n, -1, keepdims=True)) * s


def attn_kernel(acc_ref, qg_ref, kg_ref, *rest):
    out_ref, sum_ref = rest[-2:]
    scale = DH ** (-0.5)
    t1 = jnp.zeros((ROWS, DH), F32)
    t2 = jnp.zeros((ROWS, DH), F32)
    for hd in range(HW // DH):
        cols = [slice(j * HW + hd * DH, j * HW + (hd + 1) * DH) for j in range(4)]
        sl = cols[0]
        qg = qg_ref[:, sl]
        kg = kg_ref[:, sl]
        proj = [acc_ref[:ROWS, c] for c in cols]
        qn, qs = head_stats(proj[0])
        kn, ks = head_stats(proj[1])
        q = (qn * qg).astype(BF)
        k = (kn * kg).astype(BF)
        v = proj[2].astype(BF)
        ga = proj[3].astype(BF)
        e = jnp.exp(dot(q, k, 1, 1) * scale)
        p = e / jnp.sum(e, -1, keepdims=True)
        pw = p.astype(BF)
        out_ref[:, cols[3]] = dot(pw, v, 1, 0).astype(BF)
        gp = dot(ga, v, 1, 1)
        delta = jnp.sum(p * gp, -1, keepdims=True)
        gs = (p * (gp - delta) * scale).astype(BF)
        gq = head_back(dot(gs, k, 1, 0), qn, qs, qg)
        gk = head_back(dot(gs, q, 0, 0), kn, ks, kg)
        gv = dot(pw, ga, 0, 0)
        for j, val in enumerate((gq, gk, gv)):
            g = val.astype(BF)
            out_ref[:, cols[j]] = g
            g = g.astype(F32)
            t1 += g * (acc_ref[ROWS : ROWS + 1, cols[j]] + acc_ref[ROWS + 1 : ROWS + 2, cols[j]])
            t2 += g * proj[j]
    ones = jnp.ones((8, DH), F32)
    total = [
        lax.dot_general(
            ones, t, (((1,), (1,)), ((), ())), precision=lax.Precision.HIGHEST, preferred_element_type=F32
        )
        for t in (t1, t2)
    ]
    row = lax.broadcasted_iota(jnp.int32, (8, ROWS), 0)
    sum_ref[...] = jnp.where(row == 0, total[0], total[1])


def core_kernel(hid_in, cot_in, w_in, qg_ref, kg_ref, *rest):
    g_ref, sum_ref, out_ref, hid, cot, w, acc, out, sems, out_sems = rest[-10:]
    groups = NDP // KSTEP
    loads = []
    for i in range(groups):
        cols = slice(i * KSTEP * SL, (i + 1) * KSTEP * SL)
        span = slice(i * KSTEP, (i + 1) * KSTEP)
        pairs = [
            (hid_in.at[:, cols], hid.at[:, cols]),
            (cot_in.at[:, cols], cot.at[:, cols]),
            (w_in.at[span], w.at[span]),
        ]
        loads.append([pltpu.make_async_copy(a, b, sems.at[i, n]) for n, (a, b) in enumerate(pairs)])
    for group in loads:
        for copy in group:
            copy.start()
    for i, group in enumerate(loads):
        for copy in group:
            copy.wait()
        cols = slice(i * KSTEP * SL, (i + 1) * KSTEP * SL)
        for j in range(4):
            rows = EXT if j < 3 else ROWS
            src = hid if j < 3 else cot
            wj = w[i * KSTEP : (i + 1) * KSTEP, j].reshape(KSTEP * SL, HW)
            new = dot(src[:, cols], wj, 1, 0)
            dst = slice(j * HW, (j + 1) * HW)
            acc[:rows, dst] = new if i == 0 else acc[:rows, dst] + new
    attn_kernel(acc, qg_ref, kg_ref, g_ref, sum_ref)
    stores = []
    for i in range(groups):
        for s in range(i * KSTEP, (i + 1) * KSTEP):
            t = 0.0
            for j in range(3):
                t = t + dot(g_ref[:, j * HW : (j + 1) * HW], w[s, j], 1, 1)
            out[s, :ROWS] = t.astype(BF)
            out[s, ROWS:] = dot(g_ref[:, 3 * HW :], w[s, 3], 1, 1).astype(BF)
        span = slice(i * KSTEP, (i + 1) * KSTEP)
        stores.append(pltpu.make_async_copy(out.at[span], out_ref.at[span], out_sems.at[i]))
        stores[-1].start()
    for copy in stores:
        copy.wait()


def core_call(hid, cot, w, qg, kg, after):
    full = lambda shape: pl.BlockSpec(shape, lambda: (0, 0))
    groups = NDP // KSTEP
    return pl.pallas_call(
        core_kernel,
        in_specs=[ANY] * 3 + [full((1, HW)), full((1, HW))] + [ANY] * len(after),
        out_specs=[full((ROWS, 4 * HW)), full((8, ROWS)), ANY],
        out_shape=[
            jax.ShapeDtypeStruct((ROWS, 4 * HW), BF),
            jax.ShapeDtypeStruct((8, ROWS), F32),
            jax.ShapeDtypeStruct((NDP, 2 * ROWS, SL), BF),
        ],
        scratch_shapes=[
            pltpu.VMEM((EXT, D), BF),
            pltpu.VMEM((ROWS, D), BF),
            pltpu.VMEM((NDP, 4, SL, HW), BF),
            pltpu.VMEM((EXT, 4 * HW), F32),
            pltpu.VMEM((NDP, 2 * ROWS, SL), BF),
            pltpu.SemaphoreType.DMA((groups, 3)),
            pltpu.SemaphoreType.DMA((groups,)),
        ],
        compiler_params=params(),
        cost_estimate=COST,
    )(hid, cot, w, qg.reshape(1, HW), kg.reshape(1, HW), *after)


def weight_kernel(part, z_ref, *refs):
    x_refs, rest = refs[:NZ], refs[NZ:]
    g_refs = rest[:2]
    i = pl.program_id(0)
    half = NDP // 2
    n = half * SUB

    def total(step):
        new, new_o = 0.0, 0.0
        for k in (0, 1):
            for h in (0, 1):
                x = x_refs[2 * (2 * step + k) + h]
                g = g_refs[k][h * half : (h + 1) * half].reshape(n, 4 * HW)
                new = new + dot(x[:, 0].reshape(n, SL), g[:, : 3 * HW], 0, 0)
                new_o = new_o + dot(x[:, 1].reshape(n, SL), g[:, 3 * HW :], 0, 0)
        return new, new_o

    if part == 0:
        acc, acc_o = rest[2:4]

        @pl.when(i == 0)
        def _():
            acc[...], acc_o[...] = total(0)

        @pl.when(i == 1)
        def _():
            new, new_o = total(1)
            acc[...] += new
            acc_o[...] += new_o
    else:
        old, old_o, dw_ref, do_ref, acc, acc_o = rest[2:8]

        @pl.when(i == 0)
        def _():
            new, new_o = total(0)
            acc[...] = old[...] + new
            acc_o[...] = old_o[...] + new_o

        @pl.when(i == 1)
        def _():
            new, new_o = total(1)
            for j in range(3):
                sl = slice(j * HW, (j + 1) * HW)
                dw_ref[j] = (acc[:, sl] + new[:, sl]).astype(BF)
            do_ref[...] = (acc_o[...] + new_o).astype(BF)


def weight_call(part, scalars, xs, g, old):
    g = g.reshape(NDP, NZ, SUB, 4 * HW)
    shapes = [(SL, 3 * HW), (SL, HW)]
    outs = [(3, SL, HW), (SL, HW)]
    zero = lambda n: (lambda i, z: (0,) * n)
    spot = lambda k: (lambda i, z: (0, (z[0] + 2 * NZ - 4 * part - 2 * i - k) % NZ, 0, 0))
    out = outs if part else shapes
    return pl.pallas_call(
        lambda *refs: weight_kernel(part, *refs),
        grid_spec=pltpu.PrefetchScalarGridSpec(
            num_scalar_prefetch=1,
            grid=(2,),
            in_specs=[pl.BlockSpec(x.shape, zero(4)) for x in xs]
            + [pl.BlockSpec((NDP, 1, SUB, 4 * HW), spot(k)) for k in (0, 1)]
            + [pl.BlockSpec(x.shape, zero(2)) for x in old],
            out_specs=[pl.BlockSpec(x, zero(len(x))) for x in out],
            scratch_shapes=[pltpu.VMEM(x, F32) for x in shapes] if part else [],
        ),
        out_shape=[jax.ShapeDtypeStruct(x, BF if part else F32) for x in out],
        compiler_params=params(),
        cost_estimate=COST,
    )(scalars, *xs, g, g, *old)


def shift(a, k):
    return lax.ppermute(a, "z", [(i, (i + k) % NZ) for i in range(NZ)])


def swap_yh(a):
    return lax.ppermute(a, "yh", [(0, 1), (1, 0)])


def ring_gather(own, hid):
    half = NDP // 2
    a, b = own[:half], own[half:]
    ra, la = order((shift(a, 1), shift(a, -1)), (hid,))
    right, left = [(ra, shift(b, 1))], [(la, shift(b, -1))]
    for _ in range(2):
        right.append(tuple(shift(x, 1) for x in right[-1]))
        left.append(tuple(shift(x, -1) for x in left[-1]))
    return [(a, b)] + right + left[::-1]


def all_sum(a):
    x = jnp.broadcast_to(a[None], (NMP,) + a.shape)
    return jnp.sum(lax.all_to_all(x, MP, 0, 0, tiled=True), 0)


def final_kernel(s_ref, mine_ref, recv_ref, sum_ref, tok_ref, mean_ref, rstd_ref, gain_ref, *refs):
    branch_ref, token_ref = refs[-2:]
    t = mine_ref[0].astype(F32) + recv_ref[...].astype(F32)
    s = jnp.transpose(sum_ref[...]) * (1.0 / D)
    rstd = rstd_ref[...]
    xhat = (tok_ref[...].astype(F32) - mean_ref[...]) * rstd
    grad = t[:ROWS] * gain_ref[...] - s[:, 0:1] - xhat * s[:, 1:2]
    token_ref[...] = (grad * rstd).astype(BF)
    branch_ref[...] = t[ROWS:].astype(BF)


def final_call(scalars, part, recv, sums, tokens, mean, rstd, gain, after):
    fixed = lambda i, s: (0, 0)
    cols = lambda i, s: (0, s[2])
    out = jax.ShapeDtypeStruct((ROWS, SL), BF)
    return pl.pallas_call(
        final_kernel,
        grid_spec=pltpu.PrefetchScalarGridSpec(
            num_scalar_prefetch=1,
            grid=(1,),
            in_specs=[
                pl.BlockSpec((1, 2 * ROWS, SL), lambda i, s: (s[1], 0, 0)),
                pl.BlockSpec((2 * ROWS, SL), fixed),
                pl.BlockSpec((8, ROWS), fixed),
                pl.BlockSpec((ROWS, SL), cols),
                pl.BlockSpec((ROWS, 1), fixed),
                pl.BlockSpec((ROWS, 1), fixed),
                pl.BlockSpec((1, SL), cols),
            ]
            + [ANY] * len(after),
            out_specs=[pl.BlockSpec((ROWS, SL), fixed)] * 2,
        ),
        out_shape=[out, out],
        compiler_params=pltpu.CompilerParams(vmem_limit_bytes=VMEM // 4),
        cost_estimate=COST,
    )(scalars, part, recv, sums, tokens, mean, rstd, gain.reshape(1, D), *after)


def local(tokens, w_qkv, w_out, layer_norm_gain, query_gain, key_gain, cotangent):
    z = lax.axis_index("z")
    yh = lax.axis_index("yh")
    scalars = jnp.stack([z, yh, z * NYH + yh]).astype(jnp.int32)

    w_own = pack_call(w_qkv, w_out)
    w = lax.all_gather(w_own, DP, axis=0)
    side = lax.psum_scatter(w_own, "c", scatter_dimension=0, tiled=True)

    hid, mean, rstd = norm_call(tokens, layer_norm_gain)
    rows = rows_call(scalars, tokens, cotangent, layer_norm_gain)
    moved = ring_gather(lax.all_to_all(rows, DP, 0, 0, tiled=True), hid)

    (ra, rb), (la, lb) = moved[3], moved[4]
    grads, sums, terms = core_call(
        hid, cotangent, w, query_gain, key_gain, moved[2] + moved[5] + (ra, lb, side)
    )
    far = shift(ra, 1), shift(lb, -1)
    terms, grads, sums = order((terms, grads, sums), far + (rb, la))
    all_grads = lax.all_gather(grads, DP, axis=0)
    part = lax.psum_scatter(
        terms.reshape(NDP * 2 * ROWS, SL), "z", scatter_dimension=0, tiled=True
    ).reshape(NYH, 2 * ROWS, SL)
    sums = all_sum(sums)
    flat = [x for pair in moved[:3] for x in pair] + [ra, rb]
    flat += [*far, la, lb] + [x for pair in moved[5:] for x in pair]
    partial = weight_call(0, scalars, flat[:NZ], all_grads, ())
    grad_w, grad_o = weight_call(1, scalars, flat[NZ:], all_grads, partial)
    (part,) = order((part,), (grad_w, sums))
    recv = swap_yh(lax.dynamic_index_in_dim(part, 1 - yh, 0, keepdims=False))
    branch, token_gradient = final_call(
        scalars, part, recv, sums, tokens, mean, rstd, layer_norm_gain, ()
    )
    return (branch, token_gradient, grad_w.transpose(1, 0, 2), grad_o)


def solution(mesh):
    fine = Mesh(mesh.devices.reshape(NX, NYL, NC, NZ, NYH), DP + MP)
    return jax.shard_map(
        local,
        mesh=fine,
        in_specs=(
            P(DP, None),
            P(DP, None, MP),
            P(DP, MP),
            P(),
            P(MP),
            P(MP),
            P(DP, None),
        ),
        out_specs=(P(DP, MP), P(DP, MP), P(DP, None, MP), P(DP, MP)),
        check_vma=False,
    )
```

```python
import jax
import jax.numpy as jnp
from jax import lax
from jax.experimental import pallas as pl
from jax.experimental.pallas import tpu as pltpu
from jax.sharding import Mesh, PartitionSpec as P

DH = 128
EPS = 1e-06
DP = ("x", "yl", "c")
MP = ("z", "yh")
NX, NYL, NC, NZ, NYH = 4, 2, 2, 8, 2
NDP, NMP = NX * NYL * NC, NZ * NYH
ROWS = 256
SL = 384
HW = 256
D = 6144
SUB = ROWS // NZ
EXT = ROWS + 16
KSTEP = 2
COST = pl.CostEstimate(flops=1000, bytes_accessed=1000, transcendentals=0)
VMEM = 52 * 1024 * 1024
BF = jnp.bfloat16
F32 = jnp.float32


def dot(a, b, ca, cb):
    return lax.dot_general(a, b, (((ca,), (cb,)), ((), ())), preferred_element_type=F32)


def params():
    return pltpu.CompilerParams(vmem_limit_bytes=VMEM)


ANY = pl.BlockSpec(memory_space=pl.ANY)


def order(xs, after):
    n = len(xs)
    return pl.pallas_call(
        lambda *refs: None,
        in_specs=[ANY] * (n + len(after)),
        out_specs=[ANY] * n,
        out_shape=[jax.ShapeDtypeStruct(x.shape, x.dtype) for x in xs],
        input_output_aliases={i: i for i in range(n)},
        cost_estimate=COST,
    )(*xs, *after)


def normalise(t):
    mean = jnp.mean(t, -1, keepdims=True)
    cen = t - mean
    rstd = lax.rsqrt(jnp.mean(cen * cen, -1, keepdims=True) + EPS)
    return cen * rstd, mean, rstd


def norm_kernel(tok_ref, gain_ref, hid_ref, mean_ref, rstd_ref):
    i = pl.program_id(0)
    blk = tok_ref.shape[0]
    gain = gain_ref[...]
    xhat, mean, rstd = normalise(tok_ref[...].astype(F32))
    hid_ref[pl.ds(pl.multiple_of(i * blk, blk), blk), :] = (xhat * gain).astype(BF)
    mean_ref[...] = mean
    rstd_ref[...] = rstd

    @pl.when(i == pl.num_programs(0) - 1)
    def _():
        hi = gain.astype(BF).astype(F32)
        row = lax.broadcasted_iota(jnp.int32, (16, D), 0)
        extra = jnp.where(row == 0, hi, jnp.where(row == 1, gain - hi, 0.0))
        hid_ref[ROWS:, :] = extra.astype(BF)


def norm_call(tokens, gain):
    blk = 64
    return pl.pallas_call(
        norm_kernel,
        grid=(ROWS // blk,),
        in_specs=[
            pl.BlockSpec((blk, D), lambda i: (i, 0)),
            pl.BlockSpec((1, D), lambda i: (0, 0)),
        ],
        out_specs=[
            pl.BlockSpec((EXT, D), lambda i: (0, 0)),
            pl.BlockSpec((blk, 1), lambda i: (i, 0)),
            pl.BlockSpec((blk, 1), lambda i: (i, 0)),
        ],
        out_shape=[
            jax.ShapeDtypeStruct((EXT, D), BF),
            jax.ShapeDtypeStruct((ROWS, 1), F32),
            jax.ShapeDtypeStruct((ROWS, 1), F32),
        ],
        compiler_params=params(),
        cost_estimate=COST,
    )(tokens, gain.reshape(1, D))


def rows_kernel(z_ref, tok_ref, cot_ref, gain_ref, out_ref):
    xhat, _, _ = normalise(tok_ref[...].astype(F32))
    hid = (xhat * gain_ref[...]).astype(BF)
    for i in range(NDP):
        out_ref[i, 0] = hid[:, i * SL : (i + 1) * SL]
        out_ref[i, 1] = cot_ref[:, i * SL : (i + 1) * SL]


def rows_call(z, tokens, cotangent, gain):
    return pl.pallas_call(
        rows_kernel,
        grid_spec=pltpu.PrefetchScalarGridSpec(
            num_scalar_prefetch=1,
            grid=(1,),
            in_specs=[
                pl.BlockSpec((SUB, D), lambda i, z: (z[0], 0)),
                pl.BlockSpec((SUB, D), lambda i, z: (z[0], 0)),
                pl.BlockSpec((1, D), lambda i, z: (0, 0)),
            ],
            out_specs=pl.BlockSpec((NDP, 2, SUB, SL), lambda i, z: (0, 0, 0, 0)),
        ),
        out_shape=jax.ShapeDtypeStruct((NDP, 2, SUB, SL), BF),
        compiler_params=params(),
        cost_estimate=COST,
    )(z, tokens, cotangent, gain.reshape(1, D))


def head_stats(u):
    cen = u - jnp.mean(u, -1, keepdims=True)
    s = lax.rsqrt(jnp.mean(cen * cen, -1, keepdims=True) + EPS)
    return cen * s, s


def head_back(g, n, s, gain):
    e = g * gain
    return (e - jnp.mean(e, -1, keepdims=True) - n * jnp.mean(e * n, -1, keepdims=True)) * s


def attn_kernel(acc_ref, qg_ref, kg_ref, *rest):
    out_ref, sum_ref = rest[-2:]
    scale = DH ** (-0.5)
    t1 = jnp.zeros((ROWS, DH), F32)
    t2 = jnp.zeros((ROWS, DH), F32)
    for hd in range(HW // DH):
        cols = [slice(j * HW + hd * DH, j * HW + (hd + 1) * DH) for j in range(4)]
        sl = cols[0]
        qg = qg_ref[:, sl]
        kg = kg_ref[:, sl]
        proj = [acc_ref[:ROWS, c] for c in cols]
        qn, qs = head_stats(proj[0])
        kn, ks = head_stats(proj[1])
        q = (qn * qg).astype(BF)
        k = (kn * kg).astype(BF)
        v = proj[2].astype(BF)
        ga = proj[3].astype(BF)
        e = jnp.exp(dot(q, k, 1, 1) * scale)
        p = e / jnp.sum(e, -1, keepdims=True)
        pw = p.astype(BF)
        out_ref[:, cols[3]] = dot(pw, v, 1, 0).astype(BF)
        gp = dot(ga, v, 1, 1)
        delta = jnp.sum(p * gp, -1, keepdims=True)
        gs = (p * (gp - delta) * scale).astype(BF)
        gq = head_back(dot(gs, k, 1, 0), qn, qs, qg)
        gk = head_back(dot(gs, q, 0, 0), kn, ks, kg)
        gv = dot(pw, ga, 0, 0)
        for j, val in enumerate((gq, gk, gv)):
            g = val.astype(BF)
            out_ref[:, cols[j]] = g
            g = g.astype(F32)
            t1 += g * (acc_ref[ROWS : ROWS + 1, cols[j]] + acc_ref[ROWS + 1 : ROWS + 2, cols[j]])
            t2 += g * proj[j]
    ones = jnp.ones((8, DH), F32)
    total = [
        lax.dot_general(
            ones, t, (((1,), (1,)), ((), ())), precision=lax.Precision.HIGHEST, preferred_element_type=F32
        )
        for t in (t1, t2)
    ]
    row = lax.broadcasted_iota(jnp.int32, (8, ROWS), 0)
    sum_ref[...] = jnp.where(row == 0, total[0], total[1])


def core_kernel(hid_in, cot_in, w_in, qg_ref, kg_ref, *rest):
    g_ref, sum_ref, out_ref, hid, cot, w, acc, out, sems, out_sems = rest[-10:]
    groups = NDP // KSTEP
    loads = []
    for i in range(groups):
        cols = slice(i * KSTEP * SL, (i + 1) * KSTEP * SL)
        span = slice(i * KSTEP, (i + 1) * KSTEP)
        pairs = [
            (hid_in.at[:, cols], hid.at[:, cols]),
            (cot_in.at[:, cols], cot.at[:, cols]),
            (w_in.at[span], w.at[span]),
        ]
        loads.append([pltpu.make_async_copy(a, b, sems.at[i, n]) for n, (a, b) in enumerate(pairs)])
    for group in loads:
        for copy in group:
            copy.start()
    for i, group in enumerate(loads):
        for copy in group:
            copy.wait()
        cols = slice(i * KSTEP * SL, (i + 1) * KSTEP * SL)
        for j in range(4):
            rows = EXT if j < 3 else ROWS
            src = hid if j < 3 else cot
            wj = w[i * KSTEP : (i + 1) * KSTEP, j].reshape(KSTEP * SL, HW)
            new = dot(src[:, cols], wj, 1, 0)
            dst = slice(j * HW, (j + 1) * HW)
            acc[:rows, dst] = new if i == 0 else acc[:rows, dst] + new
    attn_kernel(acc, qg_ref, kg_ref, g_ref, sum_ref)
    stores = []
    for i in range(groups):
        for s in range(i * KSTEP, (i + 1) * KSTEP):
            t = 0.0
            for j in range(3):
                t = t + dot(g_ref[:, j * HW : (j + 1) * HW], w[s, j], 1, 1)
            out[s, :ROWS] = t.astype(BF)
            out[s, ROWS:] = dot(g_ref[:, 3 * HW :], w[s, 3], 1, 1).astype(BF)
        span = slice(i * KSTEP, (i + 1) * KSTEP)
        stores.append(pltpu.make_async_copy(out.at[span], out_ref.at[span], out_sems.at[i]))
        stores[-1].start()
    for copy in stores:
        copy.wait()


def core_call(hid, cot, w, qg, kg, after):
    full = lambda shape: pl.BlockSpec(shape, lambda: (0, 0))
    groups = NDP // KSTEP
    return pl.pallas_call(
        core_kernel,
        in_specs=[ANY] * 3 + [full((1, HW)), full((1, HW))] + [ANY] * len(after),
        out_specs=[full((ROWS, 4 * HW)), full((8, ROWS)), ANY],
        out_shape=[
            jax.ShapeDtypeStruct((ROWS, 4 * HW), BF),
            jax.ShapeDtypeStruct((8, ROWS), F32),
            jax.ShapeDtypeStruct((NDP, 2 * ROWS, SL), BF),
        ],
        scratch_shapes=[
            pltpu.VMEM((EXT, D), BF),
            pltpu.VMEM((ROWS, D), BF),
            pltpu.VMEM((NDP, 4, SL, HW), BF),
            pltpu.VMEM((EXT, 4 * HW), F32),
            pltpu.VMEM((NDP, 2 * ROWS, SL), BF),
            pltpu.SemaphoreType.DMA((groups, 3)),
            pltpu.SemaphoreType.DMA((groups,)),
        ],
        compiler_params=params(),
        cost_estimate=COST,
    )(hid, cot, w, qg.reshape(1, HW), kg.reshape(1, HW), *after)


def weight_kernel(part, z_ref, *refs):
    x_refs, rest = refs[:NZ], refs[NZ:]
    g_refs = rest[:2]
    i = pl.program_id(0)
    half = NDP // 2
    n = half * SUB

    def total(step):
        new, new_o = 0.0, 0.0
        for k in (0, 1):
            for h in (0, 1):
                x = x_refs[2 * (2 * step + k) + h]
                g = g_refs[k][h * half : (h + 1) * half].reshape(n, 4 * HW)
                new = new + dot(x[:, 0].reshape(n, SL), g[:, : 3 * HW], 0, 0)
                new_o = new_o + dot(x[:, 1].reshape(n, SL), g[:, 3 * HW :], 0, 0)
        return new, new_o

    if part == 0:
        acc, acc_o = rest[2:4]

        @pl.when(i == 0)
        def _():
            acc[...], acc_o[...] = total(0)

        @pl.when(i == 1)
        def _():
            new, new_o = total(1)
            acc[...] += new
            acc_o[...] += new_o
    else:
        old, old_o, dw_ref, do_ref, acc, acc_o = rest[2:8]

        @pl.when(i == 0)
        def _():
            new, new_o = total(0)
            acc[...] = old[...] + new
            acc_o[...] = old_o[...] + new_o

        @pl.when(i == 1)
        def _():
            new, new_o = total(1)
            for j in range(3):
                sl = slice(j * HW, (j + 1) * HW)
                dw_ref[j] = (acc[:, sl] + new[:, sl]).astype(BF)
            do_ref[...] = (acc_o[...] + new_o).astype(BF)


def weight_call(part, scalars, xs, g, old):
    g = g.reshape(NDP, NZ, SUB, 4 * HW)
    shapes = [(SL, 3 * HW), (SL, HW)]
    outs = [(3, SL, HW), (SL, HW)]
    zero = lambda n: (lambda i, z: (0,) * n)
    spot = lambda k: (lambda i, z: (0, (z[0] + 2 * NZ - 4 * part - 2 * i - k) % NZ, 0, 0))
    out = outs if part else shapes
    return pl.pallas_call(
        lambda *refs: weight_kernel(part, *refs),
        grid_spec=pltpu.PrefetchScalarGridSpec(
            num_scalar_prefetch=1,
            grid=(2,),
            in_specs=[pl.BlockSpec(x.shape, zero(4)) for x in xs]
            + [pl.BlockSpec((NDP, 1, SUB, 4 * HW), spot(k)) for k in (0, 1)]
            + [pl.BlockSpec(x.shape, zero(2)) for x in old],
            out_specs=[pl.BlockSpec(x, zero(len(x))) for x in out],
            scratch_shapes=[pltpu.VMEM(x, F32) for x in shapes] if part else [],
        ),
        out_shape=[jax.ShapeDtypeStruct(x, BF if part else F32) for x in out],
        compiler_params=params(),
        cost_estimate=COST,
    )(scalars, *xs, g, g, *old)


def shift(a, k):
    return lax.ppermute(a, "z", [(i, (i + k) % NZ) for i in range(NZ)])


def swap_yh(a):
    return lax.ppermute(a, "yh", [(0, 1), (1, 0)])


def ring_gather(own, hid):
    half = NDP // 2
    a, b = own[:half], own[half:]
    ra, la = order((shift(a, 1), shift(a, -1)), (hid,))
    right, left = [(ra, shift(b, 1))], [(la, shift(b, -1))]
    for _ in range(2):
        right.append(tuple(shift(x, 1) for x in right[-1]))
        left.append(tuple(shift(x, -1) for x in left[-1]))
    return [(a, b)] + right + left[::-1]


def all_sum(a):
    x = jnp.broadcast_to(a[None], (NMP,) + a.shape)
    return jnp.sum(lax.all_to_all(x, MP, 0, 0, tiled=True), 0)


def final_kernel(s_ref, mine_ref, recv_ref, sum_ref, tok_ref, mean_ref, rstd_ref, gain_ref, *refs):
    branch_ref, token_ref = refs[-2:]
    t = mine_ref[0].astype(F32) + recv_ref[...].astype(F32)
    s = jnp.transpose(sum_ref[...]) * (1.0 / D)
    rstd = rstd_ref[...]
    xhat = (tok_ref[...].astype(F32) - mean_ref[...]) * rstd
    grad = t[:ROWS] * gain_ref[...] - s[:, 0:1] - xhat * s[:, 1:2]
    token_ref[...] = (grad * rstd).astype(BF)
    branch_ref[...] = t[ROWS:].astype(BF)


def final_call(scalars, part, recv, sums, tokens, mean, rstd, gain, after):
    fixed = lambda i, s: (0, 0)
    cols = lambda i, s: (0, s[2])
    out = jax.ShapeDtypeStruct((ROWS, SL), BF)
    return pl.pallas_call(
        final_kernel,
        grid_spec=pltpu.PrefetchScalarGridSpec(
            num_scalar_prefetch=1,
            grid=(1,),
            in_specs=[
                pl.BlockSpec((1, 2 * ROWS, SL), lambda i, s: (s[1], 0, 0)),
                pl.BlockSpec((2 * ROWS, SL), fixed),
                pl.BlockSpec((8, ROWS), fixed),
                pl.BlockSpec((ROWS, SL), cols),
                pl.BlockSpec((ROWS, 1), fixed),
                pl.BlockSpec((ROWS, 1), fixed),
                pl.BlockSpec((1, SL), cols),
            ]
            + [ANY] * len(after),
            out_specs=[pl.BlockSpec((ROWS, SL), fixed)] * 2,
        ),
        out_shape=[out, out],
        compiler_params=params(),
        cost_estimate=COST,
    )(scalars, part, recv, sums, tokens, mean, rstd, gain.reshape(1, D), *after)


def local(tokens, w_qkv, w_out, layer_norm_gain, query_gain, key_gain, cotangent):
    z = lax.axis_index("z")
    yh = lax.axis_index("yh")
    scalars = jnp.stack([z, yh, z * NYH + yh]).astype(jnp.int32)

    w_own = jnp.concatenate([w_qkv.transpose(1, 0, 2), w_out[None]], 0)
    w = lax.all_gather(w_own, DP, axis=0)
    side = lax.psum_scatter(w_own, "c", scatter_dimension=0, tiled=True)

    hid, mean, rstd = norm_call(tokens, layer_norm_gain)
    rows = rows_call(scalars, tokens, cotangent, layer_norm_gain)
    moved = ring_gather(lax.all_to_all(rows, DP, 0, 0, tiled=True), hid)

    (ra, rb), (la, lb) = moved[3], moved[4]
    grads, sums, terms = core_call(
        hid, cotangent, w, query_gain, key_gain, moved[2] + moved[5] + (ra, lb, side)
    )
    far = shift(ra, 1), shift(lb, -1)
    terms, grads, sums = order((terms, grads, sums), far + (rb, la))
    all_grads = lax.all_gather(grads, DP, axis=0)
    part = lax.psum_scatter(
        terms.reshape(NDP * 2 * ROWS, SL), "z", scatter_dimension=0, tiled=True
    ).reshape(NYH, 2 * ROWS, SL)
    sums = all_sum(sums)
    flat = [x for pair in moved[:3] for x in pair] + [ra, rb]
    flat += [*far, la, lb] + [x for pair in moved[5:] for x in pair]
    partial = weight_call(0, scalars, flat[:NZ], all_grads, ())
    grad_w, grad_o = weight_call(1, scalars, flat[NZ:], all_grads, partial)
    (part,) = order((part,), (grad_w, sums))
    recv = swap_yh(lax.dynamic_index_in_dim(part, 1 - yh, 0, keepdims=False))
    branch, token_gradient = final_call(
        scalars, part, recv, sums, tokens, mean, rstd, layer_norm_gain, ()
    )
    return (branch, token_gradient, grad_w.transpose(1, 0, 2), grad_o)


def solution(mesh):
    fine = Mesh(mesh.devices.reshape(NX, NYL, NC, NZ, NYH), DP + MP)
    return jax.shard_map(
        local,
        mesh=fine,
        in_specs=(
            P(DP, None),
            P(DP, None, MP),
            P(DP, MP),
            P(),
            P(MP),
            P(MP),
            P(DP, None),
        ),
        out_specs=(P(DP, MP), P(DP, MP), P(DP, None, MP), P(DP, MP)),
        check_vma=False,
    )
```
